512 devices in a mesh: ctx: 64 (over z, y), head: 8 (over x, core).
Axes of the slice: x: 4, y: 4, z: 16, core: 2. Of those that a mesh axis runs over, the one named last changes fastest.
Arguments:
- inputs: bfloat16 [8192, 4096], P('ctx', 'head'), may hold values from -6 to 6
- log_decay: float32 [64, 8192], P('head', 'ctx'), may hold values from -1 to 0
- b_proj: bfloat16 [8192, 1024], P('ctx', 'head'), may hold values from -1.25 to 1.25
- c_proj: bfloat16 [8192, 1024], P('ctx', 'head'), may hold values from -1.25 to 1.25
- grad_out: bfloat16 [8192, 4096], P('ctx', 'head'), may hold values from -0.625 to 0.625
- w_bc: bfloat16 [2, 1024, 4096], P(None, 'head'), may hold values from -0.09375 to 0.09375
Outputs:
- grad_inputs: bfloat16 [8192, 4096], P('ctx', 'head')
- grad_decay: float32 [64, 8192], P('head', 'ctx')
- grad_b: bfloat16 [8192, 1024], P('ctx', 'head')
- grad_c: bfloat16 [8192, 1024], P('ctx', 'head')
- grad_tokens: bfloat16 [8192, 4096], P(('ctx', 'head'))
The draws below stay inside these ranges and needn't reach their ends.
All inputs are finite; a program needn't handle non-finite values.
Results may differ from the reference program's by a relative error of at most 0.017.
Values may be sent and summed in bfloat16 or wider, within the bound.
No kernel may reach another device: no remote copies, remote signals or barrier semaphores. Data moves between devices by JAX's collectives and lax.ppermute only.
A program may use at most 128 MiB of HBM per device.

```python
import math
import jax
import jax.numpy as jnp
from jax import lax

D = 4096
HEAD_TOTAL = 64
P_SIZE = 64
N = 128
GROUPS = 8
TOK_DEV = 128
TOKEN_TOTAL = 8192
N_CTX = 64
N_HEAD = 8


def draw_log_decay(key, part):
    key = jax.random.fold_in(key, 11)
    key_rows = jax.random.split(key, 8)
    slow_share = 0.5
    middle_share = 0.35
    class_pick = jax.random.uniform(key_rows[0], (HEAD_TOTAL, 1))
    slow_rate = 0.5 * math.log(10.0) / TOKEN_TOTAL * jax.random.uniform(key_rows[1], (HEAD_TOTAL, 1), minval=0.2, maxval=1.0)
    middle_rate = jnp.exp(jax.random.uniform(key_rows[7], (HEAD_TOTAL, 1), minval=math.log(0.08), maxval=math.log(0.8))) / TOK_DEV
    fast_rate = jnp.exp(jax.random.uniform(key_rows[2], (HEAD_TOTAL, 1), minval=math.log(0.02), maxval=math.log(0.033)))
    baseline_rate = jnp.where(class_pick < slow_share, slow_rate, jnp.where(class_pick < slow_share + middle_share, middle_rate, fast_rate))
    block_multiplier = jnp.exp(jax.random.uniform(key_rows[3], (HEAD_TOTAL, TOKEN_TOTAL // TOK_DEV), minval=math.log(0.5), maxval=math.log(1.5)))
    block_multiplier = jnp.repeat(block_multiplier, TOK_DEV, axis=1)
    jaggedness = jax.random.uniform(key_rows[4], (HEAD_TOTAL, TOKEN_TOTAL), minval=0.5, maxval=1.5)
    spike_position = jax.random.uniform(key_rows[5], (1, TOKEN_TOTAL)) < 2.0 / TOKEN_TOTAL
    spike_magnitude = jax.random.uniform(key_rows[6], (HEAD_TOTAL, TOKEN_TOTAL), minval=0.22, maxval=0.69)
    value_rows = -(baseline_rate * block_multiplier * jaggedness) - jnp.where(spike_position, spike_magnitude, 0.0)
    return value_rows.astype(jnp.float32)


def shard_levels(stream_key, extent, shards, least, top_value):
    gain = 1.0
    for axis_at, blocks in shards:
        steps = jax.random.uniform(jax.random.fold_in(jax.random.fold_in(stream_key, 6), axis_at), (blocks,), jnp.float32, least / len(shards), top_value / len(shards))
        gain = gain * jnp.repeat(jnp.exp(steps), extent[axis_at] // blocks).reshape((-1,) + (1,) * (len(extent) - 1 - axis_at))
    return gain


def gaussian(stream_key, dims, deviation, limit, cuts=(), kind=jnp.bfloat16):
    loudness = shard_levels(stream_key, dims, cuts, -0.22, 0.18) if cuts else 1.0
    result = jax.random.normal(stream_key, dims, jnp.float32) * deviation * loudness
    return jnp.minimum(jnp.maximum(result, -limit), limit).astype(kind)


def setup_inputs(seed: int = 0) -> dict:
    seeds = jax.random.split(jax.random.key(seed), 7)
    inputs = gaussian(seeds[0], (TOKEN_TOTAL, HEAD_TOTAL * P_SIZE), 1.0, 6.0, ((0, 64), (1, 8)))
    log_decay = draw_log_decay(jax.random.fold_in(seeds[6], 71), 0)
    b_proj = gaussian(seeds[2], (TOKEN_TOTAL, GROUPS * N), (N ** -0.5), 1.25, ((0, 64), (1, 8)))
    c_proj = gaussian(seeds[3], (TOKEN_TOTAL, GROUPS * N), (N ** -0.5), 1.25, ((0, 64), (1, 8)))
    grad_out = gaussian(seeds[4], (TOKEN_TOTAL, HEAD_TOTAL * P_SIZE), (4 * (TOK_DEV * N_CTX) ** -0.5), 0.625, ((0, 64), (1, 8)))
    w_bc = gaussian(seeds[5], (2, GROUPS * N, D), D ** -0.5, 0.09375, ((1, 8),))
    return dict(inputs=inputs, log_decay=log_decay, b_proj=b_proj, c_proj=c_proj, grad_out=grad_out, w_bc=w_bc)


def block(x_vals, log_rate, b_vals, c_vals, entering):
    length = x_vals.shape[0]
    head_count = log_rate.shape[0]
    per_group = HEAD_TOTAL // GROUPS
    x_heads = x_vals.reshape(length, head_count, P_SIZE)
    b_groups = b_vals.reshape(length, -1, N)
    c_groups = c_vals.reshape(length, -1, N)
    b_heads = jnp.repeat(b_groups, per_group, axis=1)
    c_heads = jnp.repeat(c_groups, per_group, axis=1)
    cum_rate = jnp.cumsum(log_rate, axis=1)
    scores = jnp.einsum('tgn,sgn->gts', c_groups, b_groups, precision=lax.Precision.HIGHEST)
    scores = jnp.repeat(scores, per_group, axis=0)
    rows = lax.broadcasted_iota(jnp.int32, (length, length), 0)
    cols = lax.broadcasted_iota(jnp.int32, (length, length), 1)
    lower_mask = rows >= cols
    gap_log = cum_rate[:, :, None] - cum_rate[:, None, :]
    decays = jnp.where(lower_mask, jnp.exp(jnp.where(lower_mask, gap_log, 0.0)), 0.0)
    out_vals = jnp.einsum('hts,shp->thp', scores * decays, x_heads, precision=lax.Precision.HIGHEST)
    carried = jnp.einsum('thn,hnp->thp', c_heads, entering, precision=lax.Precision.HIGHEST)
    out_vals = out_vals + jnp.exp(cum_rate).T[:, :, None] * carried
    tail_decay = jnp.exp(cum_rate[:, -1:] - cum_rate)
    leaving = jnp.exp(cum_rate[:, -1])[:, None, None] * entering
    leaving = leaving + jnp.einsum('hs,shn,shp->hnp', tail_decay, b_heads, x_heads, precision=lax.Precision.HIGHEST)
    return (out_vals.reshape(length, head_count * P_SIZE), leaving)

def reference(inputs, log_decay, b_proj, c_proj, grad_out, w_bc):

    def run(x_all, rate_all, b_all, c_all):
        x_blocks = x_all.reshape(N_CTX, TOK_DEV, HEAD_TOTAL * P_SIZE)
        rate_blocks = rate_all.reshape(HEAD_TOTAL, N_CTX, TOK_DEV).transpose(1, 0, 2)
        b_blocks = b_all.reshape(N_CTX, TOK_DEV, GROUPS * N)
        c_blocks = c_all.reshape(N_CTX, TOK_DEV, GROUPS * N)
        saved_block = jax.checkpoint(block)

        def advance(state, pieces):
            out_vals, leaving = saved_block(pieces[0], pieces[1], pieces[2], pieces[3], state)
            return (leaving, out_vals)
        start_state = jnp.zeros((HEAD_TOTAL, N, P_SIZE), jnp.float32)
        _, outputs = lax.scan(advance, start_state, (x_blocks, rate_blocks, b_blocks, c_blocks))
        return outputs.reshape(TOKEN_TOTAL, HEAD_TOTAL * P_SIZE)
    _, pullback = jax.vjp(run, inputs.astype(jnp.float32), log_decay.astype(jnp.float32), b_proj.astype(jnp.float32), c_proj.astype(jnp.float32))
    input_gradient, grad_decay, grad_bf, grad_cf = pullback(grad_out.astype(jnp.float32))
    grad_b = grad_bf.astype(jnp.bfloat16)
    grad_c = grad_cf.astype(jnp.bfloat16)
    width = GROUPS * N // N_HEAD
    summed = jnp.zeros((TOKEN_TOTAL, D), jnp.float32)
    for index in range(N_HEAD):
        low = index * width
        partial_value = jnp.dot(grad_b[:, low:low + width], w_bc[0, low:low + width], preferred_element_type=jnp.float32)
        partial_value = partial_value + jnp.dot(grad_c[:, low:low + width], w_bc[1, low:low + width], preferred_element_type=jnp.float32)
        summed = summed + partial_value.astype(jnp.bfloat16).astype(jnp.float32)
    return (input_gradient.astype(jnp.bfloat16), grad_decay, grad_b, grad_c, summed.astype(jnp.bfloat16))
```

```python
import functools

import jax
import jax.numpy as jnp
from jax import lax
from jax.experimental import pallas as pl
from jax.experimental.pallas import tpu as pltpu
from jax.sharding import Mesh, PartitionSpec as P

F32 = jnp.float32
BF16 = jnp.bfloat16
P_SIZE = 64
N = 128
HEADS = 8
WIDE = HEADS * P_SIZE
LO = 8
HI = 8
ROWS = N // LO
LANES = 128
HIGHEST = lax.Precision.HIGHEST
VMEM = pl.BlockSpec(memory_space=pltpu.VMEM)
SMEM = pl.BlockSpec(memory_space=pltpu.SMEM)


def iota(shape, axis):
    return lax.broadcasted_iota(jnp.int32, shape, axis)


def matmul(a, b, precision=None):
    return lax.dot_general(
        a, b, (((1,), (0,)), ((), ())), precision=precision, preferred_element_type=F32
    )


def matmul_nt(a, b, precision=None):
    return lax.dot_general(
        a, b, (((1,), (1,)), ((), ())), precision=precision, preferred_element_type=F32
    )


def matmul_tn(a, b):
    return lax.dot_general(a, b, (((0,), (0,)), ((), ())), preferred_element_type=F32)


def cumulative(rate):
    length = rate.shape[1]
    upper = (iota((length, length), 0) <= iota((length, length), 1)).astype(F32)
    rows = matmul(rate, upper, HIGHEST)
    return rows, jnp.transpose(rows)


def widen(columns):
    pick = (iota((HEADS, WIDE), 0) == iota((HEADS, WIDE), 1) // P_SIZE).astype(F32)
    return matmul(columns, pick, HIGHEST)


def split_three(row):
    lane = iota(row.shape, 1)
    first = row.astype(BF16).astype(F32)
    rest = row - first
    second = rest.astype(BF16).astype(F32)
    third = rest - second
    parts = jnp.where(lane < HEADS, first, jnp.where(lane < 2 * HEADS, second, third))
    return jnp.where(lane < 3 * HEADS, parts, 0.0).astype(BF16)


def join_three(rows):
    lane, column = iota((LANES, WIDE), 0), iota((LANES, WIDE), 1)
    pick = jnp.logical_and(lane % HEADS == column // P_SIZE, lane < 3 * HEADS)
    return matmul(rows, pick.astype(BF16))


def states_kernel(x_ref, rate_ref, b_ref, c_ref, g_ref, out_ref):
    _, columns = cumulative(rate_ref[...])
    wide = widen(columns)
    length = wide.shape[0]
    last = wide[length - 1 : length]
    scaled_inputs = (x_ref[...].astype(F32) * jnp.exp(last - wide)).astype(BF16)
    scaled_grads = (g_ref[...].astype(F32) * jnp.exp(wide)).astype(BF16)
    state = matmul_tn(b_ref[...], scaled_inputs).astype(BF16)
    grad = matmul_tn(c_ref[...], scaled_grads).astype(BF16)
    repeat = (iota((HEADS, LANES), 1) % HEADS == iota((HEADS, LANES), 0)).astype(F32)
    total = matmul(columns[length - 1 : length], repeat, HIGHEST)
    total = jnp.broadcast_to(split_three(total), (2 * ROWS, LANES))
    for block in range(LO):
        rows = slice(block * ROWS, (block + 1) * ROWS)
        out_ref[block, 0:ROWS, 0:WIDE] = state[rows]
        out_ref[block, ROWS : 2 * ROWS, 0:WIDE] = grad[rows]
        out_ref[block, :, WIDE : WIDE + LANES] = total


def totals_of(ref):
    rows = [ref[k, 0:ROWS, WIDE : WIDE + LANES].astype(F32)[0:1] for k in range(ref.shape[0])]
    rows = jnp.concatenate(rows, axis=0)
    return rows, join_three(rows.astype(BF16))


def segment_kernel(me_ref, in_ref, out_ref):
    me = me_ref[0]
    rows, wide = totals_of(in_ref)
    decay = jnp.exp(wide)
    state = jnp.zeros((ROWS, WIDE), F32)
    grad = jnp.zeros((ROWS, WIDE), F32)
    for k in range(LO):
        state = decay[k : k + 1] * state + in_ref[k, 0:ROWS, 0:WIDE].astype(F32)
        j = LO - 1 - k
        grad = decay[j : j + 1] * grad + in_ref[j, ROWS : 2 * ROWS, 0:WIDE].astype(F32)
    lane, other = iota((LANES, LANES), 0), iota((LANES, LANES), 1)
    fold = jnp.logical_and(lane % HEADS == other % HEADS, lane < 3 * HEADS).astype(F32)
    total = jnp.sum(matmul(rows, fold, HIGHEST), axis=0, keepdims=True)
    total = jnp.broadcast_to(split_three(total), (ROWS, LANES))
    state = state.astype(BF16)
    grad = grad.astype(BF16)
    for k in range(HI):
        out_ref[k, :, 0:WIDE] = jnp.where(k > me, state, grad)
        out_ref[k, :, WIDE : WIDE + LANES] = total


def entering_kernel(me_ref, far_ref, near_ref, out_ref):
    me = me_ref[0]
    far = jnp.exp(totals_of(far_ref)[1])
    near = jnp.exp(totals_of(near_ref)[1])
    state = jnp.zeros((ROWS, WIDE), F32)
    grad = jnp.zeros((ROWS, WIDE), F32)
    for k in range(HI):
        new = far[k : k + 1] * state + far_ref[k, :, 0:WIDE].astype(F32)
        state = jnp.where(k < me, new, state)
        j = HI - 1 - k
        new = far[j : j + 1] * grad + far_ref[j, :, 0:WIDE].astype(F32)
        grad = jnp.where(j > me, new, grad)
    for k in range(LO):
        out_ref[k, 0:ROWS, :] = state.astype(BF16)
        state = near[k : k + 1] * state + near_ref[k, 0:ROWS, 0:WIDE].astype(F32)
        j = LO - 1 - k
        out_ref[j, ROWS : 2 * ROWS, :] = grad.astype(BF16)
        grad = near[j : j + 1] * grad + near_ref[j, ROWS : 2 * ROWS, 0:WIDE].astype(F32)


def block_kernel(
    x_ref, rate_ref, b_ref, c_ref, g_ref, gx_ref, gd_ref, gb_ref, gc_ref, sx_ref, sg_ref, tail_ref, all_ref
):
    rows, columns = cumulative(rate_ref[...])
    length = columns.shape[0]
    wide = widen(columns)
    last = wide[length - 1 : length]
    tail = jnp.exp(last - wide)
    tail_ref[...] = tail
    all_ref[...] = jnp.broadcast_to(jnp.exp(last), all_ref.shape)
    sx_ref[...] = (x_ref[...].astype(F32) * tail).astype(BF16)
    sg_ref[...] = (g_ref[...].astype(F32) * jnp.exp(wide)).astype(BF16)
    b, c = b_ref[...], c_ref[...]
    scores = matmul_nt(b, c)
    source, target = iota((length, length), 0), iota((length, length), 1)
    lower = source <= target
    before = source < target
    after = (source >= target).astype(BF16)
    lane = iota((length, LANES), 1)
    grad_scores = jnp.zeros((length, length), F32)
    decay_rows = []
    for pair in range(HEADS // 2):
        at = slice(pair * LANES, (pair + 1) * LANES)
        x_pair, g_pair = x_ref[:, at], g_ref[:, at]
        weights, masked = [], []
        for side in range(2):
            head = 2 * pair + side
            mine = (lane < P_SIZE) if side == 0 else (lane >= P_SIZE)
            x_mine = jnp.where(mine, x_pair, jnp.zeros_like(x_pair))
            g_mine = jnp.where(mine, g_pair, jnp.zeros_like(g_pair))
            gap = rows[head : head + 1, :] - columns[:, head : head + 1]
            decay = jnp.where(lower, jnp.exp(jnp.where(lower, gap, 0.0)), 0.0)
            grad_weights = matmul_nt(x_mine, g_pair)
            weight = scores * decay
            grad_scores = grad_scores + grad_weights * decay
            product = (grad_weights * weight).astype(BF16)
            through = matmul(product, after)
            decay_rows.append(jnp.sum(jnp.where(before, through, 0.0), axis=0, keepdims=True))
            weights.append(weight.astype(BF16))
            masked.append(g_mine)
        gx_ref[:, at] = matmul(jnp.concatenate(weights, axis=1), jnp.concatenate(masked, axis=0))
    gd_ref[...] = jnp.concatenate(decay_rows, axis=0)
    gb_ref[...] = matmul(grad_scores.astype(BF16), c)
    gc_ref[...] = matmul(jnp.transpose(grad_scores).astype(BF16), b)


def carried_kernel(
    core_ref,
    state_ref,
    x_ref,
    b_ref,
    c_ref,
    gx_ref,
    gd_ref,
    gb_ref,
    gc_ref,
    sx_ref,
    sg_ref,
    tail_ref,
    all_ref,
    w_ref,
    out_x_ref,
    out_d_ref,
    out_b_ref,
    out_c_ref,
    keep_ref,
    send_ref,
    w_vmem,
    w_sem,
):
    fetch = pltpu.make_async_copy(w_ref, w_vmem, w_sem)
    fetch.start()
    length = x_ref.shape[0]
    state = state_ref[:, 0:ROWS, :].reshape(N, WIDE)
    grad = state_ref[:, ROWS : 2 * ROWS, :].reshape(N, WIDE)
    sx, sg = sx_ref[...], sg_ref[...]
    grad_c = (matmul_nt(sg, state) + gc_ref[...]).astype(BF16)
    grad_b = (matmul_nt(sx, grad) + gb_ref[...]).astype(BF16)
    out_b_ref[...] = grad_b
    out_c_ref[...] = grad_c
    from_state = matmul(c_ref[...], state)
    state_back = matmul(b_ref[...], grad)
    out_x_ref[...] = (gx_ref[...] + tail_ref[...] * state_back).astype(BF16)
    pick = (iota((HEADS, WIDE), 0) == iota((HEADS, WIDE), 1) // P_SIZE).astype(F32)
    through_head = matmul_nt(pick, sg.astype(F32) * from_state, HIGHEST)
    through_tail = matmul_nt(pick, sx.astype(F32) * state_back, HIGHEST)
    whole = jnp.sum(grad.astype(F32) * state.astype(F32), axis=0, keepdims=True) * all_ref[...]
    whole = jnp.sum(pick * whole, axis=1, keepdims=True)
    one, two = iota((length, length), 0), iota((length, length), 1)
    out_d_ref[...] = (
        gd_ref[...]
        + matmul(through_head, (one >= two).astype(F32), HIGHEST)
        + matmul(through_tail, (one < two).astype(F32), HIGHEST)
        + whole
    )
    both = jnp.concatenate([grad_b, grad_c], axis=1)
    sixteen = length // 8
    even = jnp.concatenate([both[2 * k * sixteen : (2 * k + 1) * sixteen] for k in range(4)], axis=0)
    odd = jnp.concatenate([both[(2 * k + 1) * sixteen : (2 * k + 2) * sixteen] for k in range(4)], axis=0)
    first = core_ref[0] == 0
    keep = jnp.where(first, even, odd)
    send = jnp.where(first, odd, even)
    both = jnp.concatenate([keep, send], axis=0)
    half = length // 2
    fetch.wait()
    step = 512
    for k in range(w_ref.shape[1] // step):
        at = slice(k * step, (k + 1) * step)
        part = matmul(both, w_vmem[:, at]).astype(BF16)
        keep_ref[:, at] = part[:half]
        send_ref[:, at] = part[half:]


def struct(shape, dtype):
    return jax.ShapeDtypeStruct(shape, dtype)


def call(kernel, out, operands, name, specs=None, scratch=(), flops=0, moved=0):
    return pl.pallas_call(
        kernel,
        out_shape=out,
        in_specs=specs or [VMEM] * len(operands),
        out_specs=jax.tree.map(lambda _: VMEM, out),
        scratch_shapes=list(scratch),
        cost_estimate=pl.CostEstimate(flops=flops, bytes_accessed=moved, transcendentals=0),
        compiler_params=pltpu.CompilerParams(vmem_limit_bytes=24 * 2**20),
        name=name,
    )(*operands)


def local(inputs, log_decay, b_proj, c_proj, grad_out, w_bc):
    length = inputs.shape[0]
    width = w_bc.shape[2]
    hi = lax.axis_index("hi").astype(jnp.int32).reshape(1)
    core = lax.axis_index("core").astype(jnp.int32).reshape(1)
    near = call(
        states_kernel,
        struct((LO, 2 * ROWS, WIDE + LANES), BF16),
        (inputs, log_decay, b_proj, c_proj, grad_out),
        "states",
        flops=4 * length * N * WIDE,
        moved=2**20,
    )
    near = lax.all_to_all(near, "lo", 0, 0)
    far = call(
        segment_kernel,
        struct((HI, ROWS, WIDE + LANES), BF16),
        (hi, near),
        "segment",
        specs=[SMEM, VMEM],
        moved=2**19,
    )
    far = lax.all_to_all(far, "hi", 0, 0)
    inside = call(
        block_kernel,
        (
            struct((length, WIDE), F32),
            struct((HEADS, length), F32),
            struct((length, N), F32),
            struct((length, N), F32),
            struct((length, WIDE), BF16),
            struct((length, WIDE), BF16),
            struct((length, WIDE), F32),
            struct((HEADS, WIDE), F32),
        ),
        (inputs, log_decay, b_proj, c_proj, grad_out),
        "block",
        flops=2**30,
        moved=4 * 2**20,
    )
    states = call(
        entering_kernel,
        struct((LO, 2 * ROWS, WIDE), BF16),
        (hi, far, near),
        "entering",
        specs=[SMEM, VMEM, VMEM],
        moved=2**19,
    )
    states = lax.all_to_all(states, "lo", 0, 0)
    operands = (core, states, inputs, b_proj, c_proj) + tuple(inside) + (w_bc.reshape(2 * N, width),)
    grad_inputs, grad_decay, grad_b, grad_c, keep, send = call(
        carried_kernel,
        (
            struct((length, WIDE), BF16),
            struct((HEADS, length), F32),
            struct((length, N), BF16),
            struct((length, N), BF16),
            struct((length // 2, width), BF16),
            struct((length // 2, width), BF16),
        ),
        operands,
        "carried",
        specs=[SMEM] + [VMEM] * (len(operands) - 2) + [pl.BlockSpec(memory_space=pl.ANY)],
        scratch=(pltpu.VMEM((2 * N, width), BF16), pltpu.SemaphoreType.DMA),
        flops=2**29,
        moved=4 * 2**20,
    )
    other = lax.ppermute(send, "core", [(0, 1), (1, 0)])
    pair = (keep.astype(F32) + other.astype(F32)).astype(BF16)
    blocks = lax.all_to_all(pair.reshape(4, length // 8, width), "x", 0, 0)
    grad_tokens = jnp.sum(blocks.astype(F32), axis=0).astype(BF16)
    return grad_inputs, grad_decay, grad_b, grad_c, grad_tokens


def solution(mesh):
    fine = Mesh(mesh.devices.reshape(HI, LO, 4, 2), ("hi", "lo", "x", "core"))
    ctx, head = ("hi", "lo"), ("x", "core")
    return jax.shard_map(
        local,
        mesh=fine,
        in_specs=(P(ctx, head), P(head, ctx), P(ctx, head), P(ctx, head), P(ctx, head), P(None, head, None)),
        out_specs=(P(ctx, head), P(head, ctx), P(ctx, head), P(ctx, head), P(ctx + head, None)),
        check_vma=False,
    )
```

```python
import functools

import jax
import jax.numpy as jnp
from jax import lax
from jax.experimental import pallas as pl
from jax.experimental.pallas import tpu as pltpu
from jax.sharding import Mesh, PartitionSpec as P

F32 = jnp.float32
BF16 = jnp.bfloat16
P_SIZE = 64
N = 128
HEADS = 8
WIDE = HEADS * P_SIZE
LO = 8
HI = 8
LANES = 128
ROWS = N // LO
HIGHEST = lax.Precision.HIGHEST
GROUPS = WIDE // LANES
STATE = GROUPS * ROWS
NEAR = 2 * STATE + 16
FAR = STATE + 16
FIRST = 4
ORDER = [(k + FIRST) & (HI - 1) for k in range(HI)]
VMEM = pl.BlockSpec(memory_space=pltpu.VMEM)
HBM = pl.BlockSpec(memory_space=pltpu.HBM)
SMEM = pl.BlockSpec(memory_space=pltpu.SMEM)


def iota(shape, axis):
    return lax.broadcasted_iota(jnp.int32, shape, axis)


def matmul(a, b, precision=None):
    return lax.dot_general(
        a, b, (((1,), (0,)), ((), ())), precision=precision, preferred_element_type=F32
    )


def matmul_nt(a, b, precision=None):
    return lax.dot_general(
        a, b, (((1,), (1,)), ((), ())), precision=precision, preferred_element_type=F32
    )


def matmul_tn(a, b):
    return lax.dot_general(a, b, (((0,), (0,)), ((), ())), preferred_element_type=F32)


def cumulative(rate):
    length = rate.shape[1]
    upper = (iota((length, length), 0) <= iota((length, length), 1)).astype(F32)
    rows = matmul(rate, upper, HIGHEST)
    return rows, jnp.transpose(rows)


def widen(columns):
    pick = (iota((HEADS, WIDE), 0) == iota((HEADS, WIDE), 1) >> 6).astype(F32)
    return matmul(columns, pick, HIGHEST)


def split_three(row):
    lane = iota(row.shape, 1)
    first = row.astype(BF16).astype(F32)
    rest = row - first
    second = rest.astype(BF16).astype(F32)
    third = rest - second
    parts = jnp.where(lane < HEADS, first, jnp.where(lane < 2 * HEADS, second, third))
    return jnp.where(lane < 3 * HEADS, parts, 0.0).astype(BF16)


def join_three(rows):
    lane, column = iota((LANES, WIDE), 0), iota((LANES, WIDE), 1)
    pick = jnp.logical_and((lane & 7) == (column >> 6), lane < 3 * HEADS)
    return matmul(rows, pick.astype(BF16))


def start_copies(sources, targets, sems):
    copies = [
        pltpu.make_async_copy(source, target, sems.at[k])
        for k, (source, target) in enumerate(zip(sources, targets))
    ]
    for copy in copies:
        copy.start()
    return copies


def states_kernel(rate_in, x_in, g_in, b_in, c_in, out_ref, rate_ref, x_ref, g_ref, b_ref, c_ref, sems):
    copies = start_copies(
        (rate_in, x_in, g_in, b_in, c_in), (rate_ref, x_ref, g_ref, b_ref, c_ref), sems
    )
    copies[0].wait()
    _, columns = cumulative(rate_ref[...])
    wide = widen(columns)
    length = wide.shape[0]
    last = wide[length - 1 : length]
    repeat = ((iota((HEADS, LANES), 1) & 7) == iota((HEADS, LANES), 0)).astype(F32)
    total = matmul(columns[length - 1 : length], repeat, HIGHEST)
    total = jnp.broadcast_to(split_three(total), (NEAR - 2 * STATE, LANES))
    tail = jnp.exp(last - wide)
    head = jnp.exp(wide)
    for copy in copies[1:]:
        copy.wait()
    scaled_inputs = (x_ref[...].astype(F32) * tail).astype(BF16)
    scaled_grads = (g_ref[...].astype(F32) * head).astype(BF16)
    state = matmul_tn(b_ref[...], scaled_inputs).astype(BF16)
    grad = matmul_tn(c_ref[...], scaled_grads).astype(BF16)
    for block in range(LO):
        rows = slice(block * ROWS, (block + 1) * ROWS)
        for k in range(GROUPS):
            at = slice(k * LANES, (k + 1) * LANES)
            out_ref[block, k * ROWS : (k + 1) * ROWS, :] = state[rows, at]
            out_ref[block, STATE + k * ROWS : STATE + (k + 1) * ROWS, :] = grad[rows, at]
        out_ref[block, 2 * STATE : NEAR, :] = total


def totals_of(ref, row):
    rows = [ref[k, row : row + 16, :].astype(F32)[0:1] for k in range(ref.shape[0])]
    rows = jnp.concatenate(rows, axis=0)
    return rows, join_three(rows.astype(BF16))


def chunk_decays(wide):
    decay = jnp.exp(wide)
    return [
        jnp.concatenate(
            [
                jnp.broadcast_to(decay[k : k + 1, j * LANES : (j + 1) * LANES], (ROWS, LANES))
                for j in range(GROUPS)
            ],
            axis=0,
        )
        for k in range(decay.shape[0])
    ]


def segment_kernel(me_ref, in_ref, out_ref):
    me = me_ref[0]
    rows, wide = totals_of(in_ref, 2 * STATE)
    decay = chunk_decays(wide)
    state = jnp.zeros((STATE, LANES), F32)
    grad = jnp.zeros((STATE, LANES), F32)
    for k in range(LO):
        state = decay[k] * state + in_ref[k, 0:STATE, :].astype(F32)
        j = LO - 1 - k
        grad = decay[j] * grad + in_ref[j, STATE : 2 * STATE, :].astype(F32)
    lane, other = iota((LANES, LANES), 0), iota((LANES, LANES), 1)
    fold = jnp.logical_and((lane & 7) == (other & 7), lane < 3 * HEADS).astype(F32)
    total = jnp.sum(matmul(rows, fold, HIGHEST), axis=0, keepdims=True)
    total = jnp.broadcast_to(split_three(total), (FAR - STATE, LANES))
    state = state.astype(BF16)
    grad = grad.astype(BF16)
    for k, segment in enumerate(ORDER):
        out_ref[k, 0:STATE, :] = jnp.where(segment > me, state, grad)
        out_ref[k, STATE:FAR, :] = total


def entering_kernel(me_ref, far_ref, near_ref, out_ref):
    me = me_ref[0]
    far = chunk_decays(totals_of(far_ref, STATE)[1])
    near = chunk_decays(totals_of(near_ref, 2 * STATE)[1])
    state = jnp.zeros((STATE, LANES), F32)
    grad = jnp.zeros((STATE, LANES), F32)
    for k in range(HI):
        at = ORDER.index(k)
        new = far[at] * state + far_ref[at, 0:STATE, :].astype(F32)
        state = jnp.where(k < me, new, state)
        j = HI - 1 - k
        at = ORDER.index(j)
        new = far[at] * grad + far_ref[at, 0:STATE, :].astype(F32)
        grad = jnp.where(j > me, new, grad)
    for k in range(LO):
        out_ref[k, 0:STATE, :] = state.astype(BF16)
        state = near[k] * state + near_ref[k, 0:STATE, :].astype(F32)
        j = LO - 1 - k
        out_ref[j, STATE : 2 * STATE, :] = grad.astype(BF16)
        grad = near[j] * grad + near_ref[j, STATE : 2 * STATE, :].astype(F32)


def block_kernel(
    rate_ref,
    x_ref,
    g_ref,
    b_ref,
    c_ref,
    gx_ref,
    gd_ref,
    gb_ref,
    gc_ref,
    sx_ref,
    sg_ref,
    tail_ref,
    all_ref,
):
    rows, columns = cumulative(rate_ref[...])
    length = columns.shape[0]
    wide = widen(columns)
    last = wide[length - 1 : length]
    tail = jnp.exp(last - wide)
    tail_ref[...] = tail
    all_ref[...] = jnp.broadcast_to(jnp.exp(last), all_ref.shape)
    sx_ref[...] = (x_ref[...].astype(F32) * tail).astype(BF16)
    sg_ref[...] = (g_ref[...].astype(F32) * jnp.exp(wide)).astype(BF16)
    b, c = b_ref[...], c_ref[...]
    scores = matmul_nt(b, c)
    source, target = iota((length, length), 0), iota((length, length), 1)
    lower = source <= target
    before = source < target
    after = (source >= target).astype(BF16)
    lane = iota((length, LANES), 1)
    grad_scores = jnp.zeros((length, length), F32)
    decay_rows = []
    for pair in range(HEADS // 2):
        at = slice(pair * LANES, (pair + 1) * LANES)
        x_pair, g_pair = x_ref[:, at], g_ref[:, at]
        weights, masked = [], []
        for side in range(2):
            head = 2 * pair + side
            mine = (lane < P_SIZE) if side == 0 else (lane >= P_SIZE)
            x_mine = jnp.where(mine, x_pair, jnp.zeros_like(x_pair))
            g_mine = jnp.where(mine, g_pair, jnp.zeros_like(g_pair))
            gap = rows[head : head + 1, :] - columns[:, head : head + 1]
            decay = jnp.where(lower, jnp.exp(jnp.where(lower, gap, 0.0)), 0.0)
            grad_weights = matmul_nt(x_mine, g_pair)
            weight = scores * decay
            grad_scores = grad_scores + grad_weights * decay
            product = (grad_weights * weight).astype(BF16)
            through = matmul(product, after)
            decay_rows.append(jnp.sum(jnp.where(before, through, 0.0), axis=0, keepdims=True))
            weights.append(weight.astype(BF16))
            masked.append(g_mine)
        gx_ref[:, at] = matmul(jnp.concatenate(weights, axis=1), jnp.concatenate(masked, axis=0))
    gd_ref[...] = jnp.concatenate(decay_rows, axis=0)
    gb_ref[...] = matmul(grad_scores.astype(BF16), c)
    gc_ref[...] = matmul(jnp.transpose(grad_scores).astype(BF16), b)


def carried_kernel(
    core_ref,
    state_ref,
    gx_ref,
    gd_ref,
    gb_ref,
    gc_ref,
    sx_ref,
    sg_ref,
    tail_ref,
    all_ref,
    b_in,
    c_in,
    w_in,
    out_x_ref,
    out_d_ref,
    out_b_ref,
    out_c_ref,
    keep_ref,
    send_ref,
    b_ref,
    c_ref,
    w_vmem,
    sems,
):
    copies = start_copies((b_in, c_in, w_in), (b_ref, c_ref, w_vmem), sems)
    length = sx_ref.shape[0]

    def whole_state(row):
        parts = [
            state_ref[:, row + k * ROWS : row + (k + 1) * ROWS, :].reshape(N, LANES)
            for k in range(GROUPS)
        ]
        return jnp.concatenate(parts, axis=1)

    state, grad = whole_state(0), whole_state(STATE)
    sx, sg = sx_ref[...], sg_ref[...]
    grad_c = (matmul_nt(sg, state) + gc_ref[...]).astype(BF16)
    grad_b = (matmul_nt(sx, grad) + gb_ref[...]).astype(BF16)
    out_b_ref[...] = grad_b
    out_c_ref[...] = grad_c
    copies[0].wait()
    copies[1].wait()
    from_state = matmul(c_ref[...], state)
    state_back = matmul(b_ref[...], grad)
    out_x_ref[...] = (gx_ref[...] + tail_ref[...] * state_back).astype(BF16)
    pick = (iota((HEADS, WIDE), 0) == iota((HEADS, WIDE), 1) >> 6).astype(F32)
    through_head = matmul_nt(pick, sg.astype(F32) * from_state, HIGHEST)
    through_tail = matmul_nt(pick, sx.astype(F32) * state_back, HIGHEST)
    whole = jnp.sum(grad.astype(F32) * state.astype(F32), axis=0, keepdims=True) * all_ref[...]
    whole = jnp.sum(pick * whole, axis=1, keepdims=True)
    one, two = iota((length, length), 0), iota((length, length), 1)
    out_d_ref[...] = (
        gd_ref[...]
        + matmul(through_head, (one >= two).astype(F32), HIGHEST)
        + matmul(through_tail, (one < two).astype(F32), HIGHEST)
        + whole
    )
    both = jnp.concatenate([grad_b, grad_c], axis=1)
    sixteen = length // 8
    even = jnp.concatenate([both[2 * k * sixteen : (2 * k + 1) * sixteen] for k in range(4)], axis=0)
    odd = jnp.concatenate([both[(2 * k + 1) * sixteen : (2 * k + 2) * sixteen] for k in range(4)], axis=0)
    first = core_ref[0] == 0
    keep = jnp.where(first, even, odd)
    send = jnp.where(first, odd, even)
    both = jnp.concatenate([keep, send], axis=0)
    half = length // 2
    copies[2].wait()
    step = 512
    for k in range(w_vmem.shape[1] // step):
        at = slice(k * step, (k + 1) * step)
        part = matmul(both, w_vmem[:, at]).astype(BF16)
        keep_ref[:, at] = part[:half]
        send_ref[:, at] = part[half:]


def struct(shape, dtype):
    return jax.ShapeDtypeStruct(shape, dtype)


def call(kernel, out, operands, name, specs=None, scratch=(), flops=0, moved=0, limit=24):
    return pl.pallas_call(
        kernel,
        out_shape=out,
        in_specs=specs or [VMEM] * len(operands),
        out_specs=jax.tree.map(lambda _: VMEM, out),
        scratch_shapes=list(scratch),
        cost_estimate=pl.CostEstimate(flops=flops, bytes_accessed=moved, transcendentals=0),
        compiler_params=pltpu.CompilerParams(vmem_limit_bytes=limit * 2**20),
        name=name,
    )(*operands)


def local(inputs, log_decay, b_proj, c_proj, grad_out, w_bc):
    length = inputs.shape[0]
    width = w_bc.shape[2]
    hi = lax.axis_index("hi").astype(jnp.int32).reshape(1)
    core = lax.axis_index("core").astype(jnp.int32).reshape(1)
    block = (log_decay, inputs, grad_out, b_proj, c_proj)
    held = [pltpu.VMEM(part.shape, part.dtype) for part in block]
    near = call(
        states_kernel,
        struct((LO, NEAR, LANES), BF16),
        block,
        "states",
        specs=[HBM] * 5,
        scratch=held + [pltpu.SemaphoreType.DMA((5,))],
        flops=4 * length * N * WIDE,
        moved=2**20,
        limit=60,
    )
    near = lax.all_to_all(near, "lo", 0, 0)
    far = call(
        segment_kernel,
        struct((HI, FAR, LANES), BF16),
        (hi, near),
        "segment",
        specs=[SMEM, VMEM],
        moved=2**19,
    )
    far = lax.all_to_all(far, "hi", 0, 0, axis_index_groups=[ORDER])
    inside = call(
        block_kernel,
        (
            struct((length, WIDE), F32),
            struct((HEADS, length), F32),
            struct((length, N), F32),
            struct((length, N), F32),
            struct((length, WIDE), BF16),
            struct((length, WIDE), BF16),
            struct((length, WIDE), F32),
            struct((HEADS, WIDE), F32),
        ),
        block,
        "block",
        flops=2**30,
        moved=4 * 2**20,
    )
    far, inside = lax.optimization_barrier((far, inside))
    states = call(
        entering_kernel,
        struct((LO, 2 * STATE, LANES), BF16),
        (hi, far, near),
        "entering",
        specs=[SMEM, VMEM, VMEM],
        moved=2**19,
    )
    states = lax.all_to_all(states, "lo", 0, 0)
    operands = (core, states) + tuple(inside) + (b_proj, c_proj, w_bc.reshape(2 * N, width))
    grad_inputs, grad_decay, grad_b, grad_c, keep, send = call(
        carried_kernel,
        (
            struct((length, WIDE), BF16),
            struct((HEADS, length), F32),
            struct((length, N), BF16),
            struct((length, N), BF16),
            struct((length // 2, width), BF16),
            struct((length // 2, width), BF16),
        ),
        operands,
        "carried",
        specs=[SMEM] + [VMEM] * (len(operands) - 4) + [HBM] * 3,
        scratch=(
            pltpu.VMEM(b_proj.shape, BF16),
            pltpu.VMEM(c_proj.shape, BF16),
            pltpu.VMEM((2 * N, width), BF16),
            pltpu.SemaphoreType.DMA((3,)),
        ),
        flops=2**29,
        moved=4 * 2**20,
    )
    other = lax.ppermute(send, "core", [(0, 1), (1, 0)])
    pair = (keep.astype(F32) + other.astype(F32)).astype(BF16)
    blocks = lax.all_to_all(pair.reshape(4, length // 8, width), "x", 0, 0)
    grad_tokens = jnp.sum(blocks.astype(F32), axis=0).astype(BF16)
    return grad_inputs, grad_decay, grad_b, grad_c, grad_tokens


def solution(mesh):
    fine = Mesh(mesh.devices.reshape(HI, LO, 4, 2), ("hi", "lo", "x", "core"))
    ctx, head = ("hi", "lo"), ("x", "core")
    return jax.shard_map(
        local,
        mesh=fine,
        in_specs=(P(ctx, head), P(head, ctx), P(ctx, head), P(ctx, head), P(ctx, head), P(None, head, None)),
        out_specs=(P(ctx, head), P(head, ctx), P(ctx, head), P(ctx, head), P(ctx + head, None)),
        check_vma=False,
    )
```

```python
import functools

import jax
import jax.numpy as jnp
from jax import lax
from jax.experimental import pallas as pl
from jax.experimental.pallas import tpu as pltpu
from jax.sharding import Mesh, PartitionSpec as P

F32 = jnp.float32
BF16 = jnp.bfloat16
P_SIZE = 64
N = 128
HEADS = 8
WIDE = HEADS * P_SIZE
LO = 8
HI = 8
LANES = 128
ROWS = N // LO
HIGHEST = lax.Precision.HIGHEST
GROUPS = WIDE // LANES
STATE = GROUPS * ROWS
NEAR = 2 * STATE + 16
FAR = STATE + 16
NEAR_ORDER = [4, 5, 6, 7, 0, 1, 2, 3]
FAR_ORDER = [4, 5, 6, 7, 0, 1, 2, 3]
BACK_ORDER = [6, 7, 0, 1, 2, 3, 4, 5]
X_ORDER = [2, 3, 0, 1]
NEAR_ORDER_OF = [NEAR_ORDER.index(k) for k in range(LO)]
VMEM = pl.BlockSpec(memory_space=pltpu.VMEM)
HBM = pl.BlockSpec(memory_space=pltpu.HBM)
SMEM = pl.BlockSpec(memory_space=pltpu.SMEM)


def iota(shape, axis):
    return lax.broadcasted_iota(jnp.int32, shape, axis)


def matmul(a, b, precision=None):
    return lax.dot_general(
        a, b, (((1,), (0,)), ((), ())), precision=precision, preferred_element_type=F32
    )


def matmul_nt(a, b, precision=None):
    return lax.dot_general(
        a, b, (((1,), (1,)), ((), ())), precision=precision, preferred_element_type=F32
    )


def matmul_tn(a, b):
    return lax.dot_general(a, b, (((0,), (0,)), ((), ())), preferred_element_type=F32)


def cumulative(rate):
    length = rate.shape[1]
    upper = (iota((length, length), 0) <= iota((length, length), 1)).astype(F32)
    rows = matmul(rate, upper, HIGHEST)
    return rows, jnp.transpose(rows)


def widen(columns):
    pick = (iota((HEADS, WIDE), 0) == iota((HEADS, WIDE), 1) >> 6).astype(F32)
    return matmul(columns, pick, HIGHEST)


def split_three(row):
    lane = iota(row.shape, 1)
    first = row.astype(BF16).astype(F32)
    rest = row - first
    second = rest.astype(BF16).astype(F32)
    third = rest - second
    parts = jnp.where(lane < HEADS, first, jnp.where(lane < 2 * HEADS, second, third))
    return jnp.where(lane < 3 * HEADS, parts, 0.0).astype(BF16)


def join_three(rows):
    lane, column = iota((LANES, WIDE), 0), iota((LANES, WIDE), 1)
    pick = jnp.logical_and((lane & 7) == (column >> 6), lane < 3 * HEADS)
    return matmul(rows, pick.astype(BF16))


def start_copies(sources, targets, sems):
    copies = [
        pltpu.make_async_copy(source, target, sems.at[k])
        for k, (source, target) in enumerate(zip(sources, targets))
    ]
    for copy in copies:
        copy.start()
    return copies


def states_kernel(rate_in, x_in, g_in, b_in, c_in, out_ref, rate_ref, x_ref, g_ref, b_ref, c_ref, sems):
    copies = start_copies(
        (rate_in, x_in, g_in, b_in, c_in), (rate_ref, x_ref, g_ref, b_ref, c_ref), sems
    )
    copies[0].wait()
    _, columns = cumulative(rate_ref[...])
    wide = widen(columns)
    length = wide.shape[0]
    last = wide[length - 1 : length]
    repeat = ((iota((HEADS, LANES), 1) & 7) == iota((HEADS, LANES), 0)).astype(F32)
    total = matmul(columns[length - 1 : length], repeat, HIGHEST)
    total = jnp.broadcast_to(split_three(total), (NEAR - 2 * STATE, LANES))
    tail = jnp.exp(last - wide)
    head = jnp.exp(wide)
    for copy in copies[1:]:
        copy.wait()
    scaled_inputs = (x_ref[...].astype(F32) * tail).astype(BF16)
    scaled_grads = (g_ref[...].astype(F32) * head).astype(BF16)
    state = matmul_tn(b_ref[...], scaled_inputs).astype(BF16)
    grad = matmul_tn(c_ref[...], scaled_grads).astype(BF16)
    for place, block in enumerate(NEAR_ORDER):
        rows = slice(block * ROWS, (block + 1) * ROWS)
        for k in range(GROUPS):
            at = slice(k * LANES, (k + 1) * LANES)
            out_ref[place, k * ROWS : (k + 1) * ROWS, :] = state[rows, at]
            out_ref[place, STATE + k * ROWS : STATE + (k + 1) * ROWS, :] = grad[rows, at]
        out_ref[place, 2 * STATE : NEAR, :] = total


def totals_of(ref, row):
    rows = [ref[k, row : row + 16, :].astype(F32)[0:1] for k in range(ref.shape[0])]
    rows = jnp.concatenate(rows, axis=0)
    return rows, join_three(rows.astype(BF16))


def chunk_decays(wide):
    decay = jnp.exp(wide)
    return [
        jnp.concatenate(
            [
                jnp.broadcast_to(decay[k : k + 1, j * LANES : (j + 1) * LANES], (ROWS, LANES))
                for j in range(GROUPS)
            ],
            axis=0,
        )
        for k in range(decay.shape[0])
    ]


def segment_kernel(me_ref, in_ref, out_ref):
    me = me_ref[0]
    rows, wide = totals_of(in_ref, 2 * STATE)
    decay = chunk_decays(wide)
    state = jnp.zeros((STATE, LANES), F32)
    grad = jnp.zeros((STATE, LANES), F32)
    for k in NEAR_ORDER_OF:
        state = decay[k] * state + in_ref[k, 0:STATE, :].astype(F32)
    for j in reversed(NEAR_ORDER_OF):
        grad = decay[j] * grad + in_ref[j, STATE : 2 * STATE, :].astype(F32)
    lane, other = iota((LANES, LANES), 0), iota((LANES, LANES), 1)
    fold = jnp.logical_and((lane & 7) == (other & 7), lane < 3 * HEADS).astype(F32)
    total = jnp.sum(matmul(rows, fold, HIGHEST), axis=0, keepdims=True)
    total = jnp.broadcast_to(split_three(total), (FAR - STATE, LANES))
    state = state.astype(BF16)
    grad = grad.astype(BF16)
    for k, segment in enumerate(FAR_ORDER):
        out_ref[k, 0:STATE, :] = jnp.where(segment > me, state, grad)
        out_ref[k, STATE:FAR, :] = total


def entering_kernel(me_ref, far_ref, near_ref, out_ref):
    me = me_ref[0]
    far = chunk_decays(totals_of(far_ref, STATE)[1])
    near = chunk_decays(totals_of(near_ref, 2 * STATE)[1])
    state = jnp.zeros((STATE, LANES), F32)
    grad = jnp.zeros((STATE, LANES), F32)
    for k in range(HI):
        at = FAR_ORDER.index(k)
        new = far[at] * state + far_ref[at, 0:STATE, :].astype(F32)
        state = jnp.where(k < me, new, state)
        j = HI - 1 - k
        at = FAR_ORDER.index(j)
        new = far[at] * grad + far_ref[at, 0:STATE, :].astype(F32)
        grad = jnp.where(j > me, new, grad)
    for k in range(LO):
        at = NEAR_ORDER.index(k)
        out_ref[BACK_ORDER.index(k), 0:STATE, :] = state.astype(BF16)
        state = near[at] * state + near_ref[at, 0:STATE, :].astype(F32)
        k = LO - 1 - k
        j = NEAR_ORDER.index(k)
        out_ref[BACK_ORDER.index(k), STATE : 2 * STATE, :] = grad.astype(BF16)
        grad = near[j] * grad + near_ref[j, STATE : 2 * STATE, :].astype(F32)


def block_kernel(
    rate_in,
    x_in,
    g_in,
    b_in,
    c_in,
    wide_ref,
    narrow_ref,
    scaled_ref,
    rate_ref,
    x_ref,
    g_ref,
    b_ref,
    c_ref,
    sems,
):
    copies = start_copies(
        (rate_in, x_in, g_in, b_in, c_in), (rate_ref, x_ref, g_ref, b_ref, c_ref), sems
    )
    for copy in copies:
        copy.wait()
    rows, columns = cumulative(rate_ref[...])
    length = columns.shape[0]
    wide = widen(columns)
    last = wide[length - 1 : length]
    tail = jnp.exp(last - wide)
    wide_ref[length : 2 * length, :] = tail
    wide_ref[2 * length : 2 * length + 8, :] = jnp.broadcast_to(jnp.exp(last), (8, WIDE))
    scaled_ref[0:length, :] = (x_ref[...].astype(F32) * tail).astype(BF16)
    scaled_ref[length : 2 * length, :] = (g_ref[...].astype(F32) * jnp.exp(wide)).astype(BF16)
    b, c = b_ref[...], c_ref[...]
    scores = matmul_nt(b, c)
    source, target = iota((length, length), 0), iota((length, length), 1)
    lower = source <= target
    before = source < target
    after = (source >= target).astype(BF16)
    lane = iota((length, LANES), 1)
    grad_scores = jnp.zeros((length, length), F32)
    decay_rows = []
    for pair in range(HEADS // 2):
        at = slice(pair * LANES, (pair + 1) * LANES)
        x_pair, g_pair = x_ref[:, at], g_ref[:, at]
        weights, masked = [], []
        for side in range(2):
            head = 2 * pair + side
            mine = (lane < P_SIZE) if side == 0 else (lane >= P_SIZE)
            x_mine = jnp.where(mine, x_pair, jnp.zeros_like(x_pair))
            g_mine = jnp.where(mine, g_pair, jnp.zeros_like(g_pair))
            gap = rows[head : head + 1, :] - columns[:, head : head + 1]
            decay = jnp.where(lower, jnp.exp(jnp.where(lower, gap, 0.0)), 0.0)
            grad_weights = matmul_nt(x_mine, g_pair)
            weight = scores * decay
            grad_scores = grad_scores + grad_weights * decay
            product = (grad_weights * weight).astype(BF16)
            through = matmul(product, after)
            decay_rows.append(jnp.sum(jnp.where(before, through, 0.0), axis=0, keepdims=True))
            weights.append(weight.astype(BF16))
            masked.append(g_mine)
        wide_ref[0:length, at] = matmul(jnp.concatenate(weights, axis=1), jnp.concatenate(masked, axis=0))
    narrow_ref[2 * length : 2 * length + HEADS, :] = jnp.concatenate(decay_rows, axis=0)
    narrow_ref[0:length, :] = matmul(grad_scores.astype(BF16), c)
    narrow_ref[length : 2 * length, :] = matmul(jnp.transpose(grad_scores).astype(BF16), b)


def carried_kernel(
    core_ref,
    state_ref,
    wide_ref,
    narrow_ref,
    scaled_ref,
    w_ref,
    b_in,
    c_in,
    out_x_ref,
    out_d_ref,
    out_b_ref,
    out_c_ref,
    keep_ref,
    send_ref,
    b_ref,
    c_ref,
    sems,
):
    copies = start_copies((b_in, c_in), (b_ref, c_ref), sems)
    length = b_ref.shape[0]
    first, second = slice(0, length), slice(length, 2 * length)
    heads = slice(2 * length, 2 * length + HEADS)

    def whole_state(row):
        parts = []
        for k in range(GROUPS):
            at = slice(row + k * ROWS, row + (k + 1) * ROWS)
            chunks = [state_ref[BACK_ORDER.index(block), at, :] for block in range(LO)]
            parts.append(jnp.concatenate(chunks, axis=0))
        return jnp.concatenate(parts, axis=1)

    state, grad = whole_state(0), whole_state(STATE)
    sx, sg = scaled_ref[first, :], scaled_ref[second, :]
    grad_c = (matmul_nt(sg, state) + narrow_ref[second, :]).astype(BF16)
    grad_b = (matmul_nt(sx, grad) + narrow_ref[first, :]).astype(BF16)
    out_b_ref[...] = grad_b
    out_c_ref[...] = grad_c
    copies[0].wait()
    copies[1].wait()
    from_state = matmul(c_ref[...], state)
    state_back = matmul(b_ref[...], grad)
    out_x_ref[...] = (wide_ref[first, :] + wide_ref[second, :] * state_back).astype(BF16)
    pick = (iota((HEADS, WIDE), 0) == iota((HEADS, WIDE), 1) >> 6).astype(F32)
    through_head = matmul_nt(pick, sg.astype(F32) * from_state, HIGHEST)
    through_tail = matmul_nt(pick, sx.astype(F32) * state_back, HIGHEST)
    whole = jnp.sum(grad.astype(F32) * state.astype(F32), axis=0, keepdims=True) * wide_ref[heads, :]
    whole = jnp.sum(pick * whole, axis=1, keepdims=True)
    one, two = iota((length, length), 0), iota((length, length), 1)
    out_d_ref[...] = (
        narrow_ref[heads, :]
        + matmul(through_head, (one >= two).astype(F32), HIGHEST)
        + matmul(through_tail, (one < two).astype(F32), HIGHEST)
        + whole
    )
    both = jnp.concatenate([grad_b, grad_c], axis=1)
    sixteen = length // 8
    even = jnp.concatenate([both[2 * k * sixteen : (2 * k + 1) * sixteen] for k in X_ORDER], axis=0)
    odd = jnp.concatenate([both[(2 * k + 1) * sixteen : (2 * k + 2) * sixteen] for k in X_ORDER], axis=0)
    here = core_ref[0] == 0
    keep = jnp.where(here, even, odd)
    send = jnp.where(here, odd, even)
    both = jnp.concatenate([keep, send], axis=0)
    half = length // 2
    step = 512
    for k in range(w_ref.shape[1] // step):
        at = slice(k * step, (k + 1) * step)
        part = matmul(both, w_ref[:, at]).astype(BF16)
        keep_ref[:, at] = part[:half]
        send_ref[:, at] = part[half:]


def struct(shape, dtype):
    return jax.ShapeDtypeStruct(shape, dtype)


def call(kernel, out, operands, name, specs=None, scratch=(), flops=0, moved=0, limit=24):
    return pl.pallas_call(
        kernel,
        out_shape=out,
        in_specs=specs or [VMEM] * len(operands),
        out_specs=jax.tree.map(lambda _: VMEM, out),
        scratch_shapes=list(scratch),
        cost_estimate=pl.CostEstimate(flops=flops, bytes_accessed=moved, transcendentals=0),
        compiler_params=pltpu.CompilerParams(vmem_limit_bytes=limit * 2**20),
        name=name,
    )(*operands)


def local(inputs, log_decay, b_proj, c_proj, grad_out, w_bc):
    length = inputs.shape[0]
    width = w_bc.shape[2]
    hi = lax.axis_index("hi").astype(jnp.int32).reshape(1)
    core = lax.axis_index("core").astype(jnp.int32).reshape(1)
    block = [
        pltpu.with_memory_space_constraint(part, pltpu.HBM)
        for part in (log_decay, inputs, grad_out, b_proj, c_proj)
    ]
    held = [pltpu.VMEM(part.shape, part.dtype) for part in block]
    near = call(
        states_kernel,
        struct((LO, NEAR, LANES), BF16),
        block,
        "states",
        specs=[HBM] * 5,
        scratch=held + [pltpu.SemaphoreType.DMA((5,))],
        flops=4 * length * N * WIDE,
        moved=2**20,
    )
    near = lax.all_to_all(near, "lo", 0, 0, axis_index_groups=[NEAR_ORDER])
    far = call(
        segment_kernel,
        struct((HI, FAR, LANES), BF16),
        (hi, near),
        "segment",
        specs=[SMEM, VMEM],
        moved=2**19,
    )
    far = lax.all_to_all(far, "hi", 0, 0, axis_index_groups=[FAR_ORDER])
    inside = call(
        block_kernel,
        (
            struct((2 * length + HEADS, WIDE), F32),
            struct((2 * length + HEADS, N), F32),
            struct((2 * length, WIDE), BF16),
        ),
        block,
        "block",
        specs=[HBM] * 5,
        scratch=held + [pltpu.SemaphoreType.DMA((5,))],
        flops=2**30,
        moved=4 * 2**20,
    )
    far, inside = lax.optimization_barrier((far, inside))
    states = call(
        entering_kernel,
        struct((LO, 2 * STATE, LANES), BF16),
        (hi, far, near),
        "entering",
        specs=[SMEM, VMEM, VMEM],
        moved=2**19,
    )
    states = lax.all_to_all(states, "lo", 0, 0, axis_index_groups=[BACK_ORDER])
    operands = (core, states) + tuple(inside) + (w_bc.reshape(2 * N, width), block[3], block[4])
    grad_inputs, grad_decay, grad_b, grad_c, keep, send = call(
        carried_kernel,
        (
            struct((length, WIDE), BF16),
            struct((HEADS, length), F32),
            struct((length, N), BF16),
            struct((length, N), BF16),
            struct((length // 2, width), BF16),
            struct((length // 2, width), BF16),
        ),
        operands,
        "carried",
        specs=[SMEM] + [VMEM] * (len(operands) - 3) + [HBM] * 2,
        scratch=(
            pltpu.VMEM(b_proj.shape, BF16),
            pltpu.VMEM(c_proj.shape, BF16),
            pltpu.SemaphoreType.DMA((2,)),
        ),
        flops=2**29,
        moved=4 * 2**20,
    )
    other = lax.ppermute(send, "core", [(0, 1), (1, 0)])
    pair = (keep.astype(F32) + other.astype(F32)).astype(BF16)
    blocks = pair.reshape(4, length // 8, width)
    blocks = lax.all_to_all(blocks, "x", 0, 0, axis_index_groups=[X_ORDER])
    grad_tokens = jnp.sum(blocks.astype(F32), axis=0).astype(BF16)
    return grad_inputs, grad_decay, grad_b, grad_c, grad_tokens


def solution(mesh):
    fine = Mesh(mesh.devices.reshape(HI, LO, 4, 2), ("hi", "lo", "x", "core"))
    ctx, head = ("hi", "lo"), ("x", "core")
    return jax.shard_map(
        local,
        mesh=fine,
        in_specs=(P(ctx, head), P(head, ctx), P(ctx, head), P(ctx, head), P(ctx, head), P(None, head, None)),
        out_specs=(P(ctx, head), P(head, ctx), P(ctx, head), P(ctx, head), P(ctx + head, None)),
        check_vma=False,
    )
```

```python
import functools

import jax
import jax.numpy as jnp
from jax import lax
from jax.experimental import pallas as pl
from jax.experimental.pallas import tpu as pltpu
from jax.sharding import Mesh, PartitionSpec as P

F32 = jnp.float32
BF16 = jnp.bfloat16
P_SIZE = 64
N = 128
HEADS = 8
WIDE = HEADS * P_SIZE
LO = 8
HI = 8
LANES = 128
ROWS = N // LO
HIGHEST = lax.Precision.HIGHEST
GROUPS = WIDE // LANES
STATE = GROUPS * ROWS
NEAR = 2 * STATE + 16
FAR = STATE + 16
NEAR_ORDER = [7, 0, 1, 2, 3, 4, 5, 6]
FAR_ORDER = [4, 5, 6, 7, 0, 1, 2, 3]
BACK_ORDER = [6, 7, 0, 1, 2, 3, 4, 5]
X_ORDER = [2, 3, 0, 1]
NEAR_ORDER_OF = [NEAR_ORDER.index(k) for k in range(LO)]
VMEM = pl.BlockSpec(memory_space=pltpu.VMEM)
HBM = pl.BlockSpec(memory_space=pltpu.HBM)


def iota(shape, axis):
    return lax.broadcasted_iota(jnp.int32, shape, axis)


def matmul(a, b, precision=None):
    return lax.dot_general(
        a, b, (((1,), (0,)), ((), ())), precision=precision, preferred_element_type=F32
    )


def matmul_nt(a, b, precision=None):
    return lax.dot_general(
        a, b, (((1,), (1,)), ((), ())), precision=precision, preferred_element_type=F32
    )


def matmul_tn(a, b):
    return lax.dot_general(a, b, (((0,), (0,)), ((), ())), preferred_element_type=F32)


def cumulative(rate):
    length = rate.shape[1]
    upper = (iota((length, length), 0) <= iota((length, length), 1)).astype(F32)
    rows = matmul(rate, upper, HIGHEST)
    return rows, jnp.transpose(rows)


def widen(columns):
    pick = (iota((HEADS, WIDE), 0) == iota((HEADS, WIDE), 1) >> 6).astype(F32)
    return matmul(columns, pick, HIGHEST)


def split_three(row):
    lane = iota(row.shape, 1)
    first = row.astype(BF16).astype(F32)
    rest = row - first
    second = rest.astype(BF16).astype(F32)
    third = rest - second
    parts = jnp.where(lane < HEADS, first, jnp.where(lane < 2 * HEADS, second, third))
    return jnp.where(lane < 3 * HEADS, parts, 0.0).astype(BF16)


def join_three(rows):
    lane, column = iota((LANES, WIDE), 0), iota((LANES, WIDE), 1)
    pick = jnp.logical_and((lane & 7) == (column >> 6), lane < 3 * HEADS)
    return matmul(rows, pick.astype(BF16))


def start_copies(sources, targets, sems):
    copies = [
        pltpu.make_async_copy(source, target, sems.at[k])
        for k, (source, target) in enumerate(zip(sources, targets))
    ]
    for copy in copies:
        copy.start()
    return copies


def states_kernel(rate_in, x_in, g_in, b_in, c_in, out_ref, rate_ref, x_ref, g_ref, b_ref, c_ref, sems):
    copies = start_copies(
        (rate_in, x_in, g_in, b_in, c_in), (rate_ref, x_ref, g_ref, b_ref, c_ref), sems
    )
    copies[0].wait()
    _, columns = cumulative(rate_ref[...])
    wide = widen(columns)
    length = wide.shape[0]
    last = wide[length - 1 : length]
    repeat = ((iota((HEADS, LANES), 1) & 7) == iota((HEADS, LANES), 0)).astype(F32)
    total = matmul(columns[length - 1 : length], repeat, HIGHEST)
    total = jnp.broadcast_to(split_three(total), (NEAR - 2 * STATE, LANES))
    tail = jnp.exp(last - wide)
    head = jnp.exp(wide)
    for copy in copies[1:]:
        copy.wait()
    scaled_inputs = (x_ref[...].astype(F32) * tail).astype(BF16)
    scaled_grads = (g_ref[...].astype(F32) * head).astype(BF16)
    state = matmul_tn(b_ref[...], scaled_inputs).astype(BF16)
    grad = matmul_tn(c_ref[...], scaled_grads).astype(BF16)
    for place, block in enumerate(NEAR_ORDER):
        rows = slice(block * ROWS, (block + 1) * ROWS)
        for k in range(GROUPS):
            at = slice(k * LANES, (k + 1) * LANES)
            out_ref[place, k * ROWS : (k + 1) * ROWS, :] = state[rows, at]
            out_ref[place, STATE + k * ROWS : STATE + (k + 1) * ROWS, :] = grad[rows, at]
        out_ref[place, 2 * STATE : NEAR, :] = total


def totals_of(ref, row):
    rows = [ref[k, row : row + 16, :].astype(F32)[0:1] for k in range(ref.shape[0])]
    rows = jnp.concatenate(rows, axis=0)
    return rows, join_three(rows.astype(BF16))


def chunk_decays(wide):
    decay = jnp.exp(wide)
    return [
        jnp.concatenate(
            [
                jnp.broadcast_to(decay[k : k + 1, j * LANES : (j + 1) * LANES], (ROWS, LANES))
                for j in range(GROUPS)
            ],
            axis=0,
        )
        for k in range(decay.shape[0])
    ]


def segment_kernel(in_ref, out_ref):
    me = lax.axis_index("hi")
    rows, wide = totals_of(in_ref, 2 * STATE)
    decay = chunk_decays(wide)
    state = jnp.zeros((STATE, LANES), F32)
    grad = jnp.zeros((STATE, LANES), F32)
    for k in NEAR_ORDER_OF:
        state = decay[k] * state + in_ref[k, 0:STATE, :].astype(F32)
    for j in reversed(NEAR_ORDER_OF):
        grad = decay[j] * grad + in_ref[j, STATE : 2 * STATE, :].astype(F32)
    lane, other = iota((LANES, LANES), 0), iota((LANES, LANES), 1)
    fold = jnp.logical_and((lane & 7) == (other & 7), lane < 3 * HEADS).astype(F32)
    total = jnp.sum(matmul(rows, fold, HIGHEST), axis=0, keepdims=True)
    total = jnp.broadcast_to(split_three(total), (FAR - STATE, LANES))
    state = state.astype(BF16)
    grad = grad.astype(BF16)
    for k, segment in enumerate(FAR_ORDER):
        out_ref[k, 0:STATE, :] = jnp.where(segment > me, state, grad)
        out_ref[k, STATE:FAR, :] = total


def entering_kernel(far_ref, near_ref, out_ref):
    me = lax.axis_index("hi")
    far = chunk_decays(totals_of(far_ref, STATE)[1])
    near = chunk_decays(totals_of(near_ref, 2 * STATE)[1])
    state = jnp.zeros((STATE, LANES), F32)
    grad = jnp.zeros((STATE, LANES), F32)
    for k in range(HI):
        at = FAR_ORDER.index(k)
        new = far[at] * state + far_ref[at, 0:STATE, :].astype(F32)
        state = jnp.where(k < me, new, state)
        j = HI - 1 - k
        at = FAR_ORDER.index(j)
        new = far[at] * grad + far_ref[at, 0:STATE, :].astype(F32)
        grad = jnp.where(j > me, new, grad)
    for k in range(LO):
        at = NEAR_ORDER.index(k)
        out_ref[BACK_ORDER.index(k), 0:STATE, :] = state.astype(BF16)
        state = near[at] * state + near_ref[at, 0:STATE, :].astype(F32)
        k = LO - 1 - k
        j = NEAR_ORDER.index(k)
        out_ref[BACK_ORDER.index(k), STATE : 2 * STATE, :] = grad.astype(BF16)
        grad = near[j] * grad + near_ref[j, STATE : 2 * STATE, :].astype(F32)


def block_kernel(
    rate_in,
    x_in,
    g_in,
    b_in,
    c_in,
    wide_ref,
    narrow_ref,
    scaled_ref,
    maps_ref,
    rate_ref,
    x_ref,
    g_ref,
    b_ref,
    c_ref,
    sems,
):
    copies = start_copies(
        (rate_in, x_in, g_in, b_in, c_in), (rate_ref, x_ref, g_ref, b_ref, c_ref), sems
    )
    for copy in copies:
        copy.wait()
    rows, columns = cumulative(rate_ref[...])
    length = columns.shape[0]
    wide = widen(columns)
    last = wide[length - 1 : length]
    tail = jnp.exp(last - wide)
    wide_ref[length : 2 * length, :] = tail
    wide_ref[2 * length : 2 * length + 8, :] = jnp.broadcast_to(jnp.exp(last), (8, WIDE))
    scaled_ref[0:length, :] = (x_ref[...].astype(F32) * tail).astype(BF16)
    scaled_ref[length : 2 * length, :] = (g_ref[...].astype(F32) * jnp.exp(wide)).astype(BF16)
    b, c = b_ref[...], c_ref[...]
    maps_ref[0:length, :] = b
    maps_ref[length : 2 * length, :] = c
    scores = matmul_nt(b, c)
    source, target = iota((length, length), 0), iota((length, length), 1)
    lower = source <= target
    before = source < target
    after = (source >= target).astype(BF16)
    lane = iota((length, LANES), 1)
    grad_scores = jnp.zeros((length, length), F32)
    decay_rows = []
    for pair in range(HEADS // 2):
        at = slice(pair * LANES, (pair + 1) * LANES)
        x_pair, g_pair = x_ref[:, at], g_ref[:, at]
        weights, masked = [], []
        for side in range(2):
            head = 2 * pair + side
            mine = (lane < P_SIZE) if side == 0 else (lane >= P_SIZE)
            x_mine = jnp.where(mine, x_pair, jnp.zeros_like(x_pair))
            g_mine = jnp.where(mine, g_pair, jnp.zeros_like(g_pair))
            gap = rows[head : head + 1, :] - columns[:, head : head + 1]
            decay = jnp.where(lower, jnp.exp(jnp.where(lower, gap, 0.0)), 0.0)
            grad_weights = matmul_nt(x_mine, g_pair)
            weight = scores * decay
            grad_scores = grad_scores + grad_weights * decay
            product = (grad_weights * weight).astype(BF16)
            through = matmul(product, after)
            decay_rows.append(jnp.sum(jnp.where(before, through, 0.0), axis=0, keepdims=True))
            weights.append(weight.astype(BF16))
            masked.append(g_mine)
        wide_ref[0:length, at] = matmul(jnp.concatenate(weights, axis=1), jnp.concatenate(masked, axis=0))
    narrow_ref[2 * length : 2 * length + HEADS, :] = jnp.concatenate(decay_rows, axis=0)
    narrow_ref[0:length, :] = matmul(grad_scores.astype(BF16), c)
    narrow_ref[length : 2 * length, :] = matmul(jnp.transpose(grad_scores).astype(BF16), b)


def whole_state(ref, row):
    parts = []
    for k in range(GROUPS):
        at = slice(row + k * ROWS, row + (k + 1) * ROWS)
        chunks = [ref[BACK_ORDER.index(block), at, :] for block in range(LO)]
        parts.append(jnp.concatenate(chunks, axis=0))
    return jnp.concatenate(parts, axis=1)


def tokens_kernel(state_ref, narrow_ref, scaled_ref, w_ref, both_ref, keep_ref, send_ref):
    length = scaled_ref.shape[0] // 2
    first, second = slice(0, length), slice(length, 2 * length)
    grad_c = matmul_nt(scaled_ref[second, :], whole_state(state_ref, 0))
    grad_b = matmul_nt(scaled_ref[first, :], whole_state(state_ref, STATE))
    grad_c = (grad_c + narrow_ref[second, :]).astype(BF16)
    grad_b = (grad_b + narrow_ref[first, :]).astype(BF16)
    both_ref[first, :] = grad_b
    both_ref[second, :] = grad_c
    both = jnp.concatenate([grad_b, grad_c], axis=1)
    rows = length // 8
    even = jnp.concatenate([both[2 * k * rows : (2 * k + 1) * rows] for k in X_ORDER], axis=0)
    odd = jnp.concatenate([both[(2 * k + 1) * rows : (2 * k + 2) * rows] for k in X_ORDER], axis=0)
    here = lax.axis_index("core") == 0
    keep = jnp.where(here, even, odd)
    send = jnp.where(here, odd, even)
    both = jnp.concatenate([keep, send], axis=0)
    half = length // 2
    step = 512
    for k in range(w_ref.shape[1] // step):
        at = slice(k * step, (k + 1) * step)
        part = matmul(both, w_ref[:, at]).astype(BF16)
        keep_ref[:, at] = part[:half]
        send_ref[:, at] = part[half:]


def sum_heads(pick, values):
    pick = pick.astype(BF16)
    high = values.astype(BF16)
    low = (values - high.astype(F32)).astype(BF16)
    return matmul_nt(pick, high) + matmul_nt(pick, low)


def carried_kernel(
    state_ref,
    wide_ref,
    narrow_ref,
    scaled_ref,
    both_ref,
    maps_ref,
    out_x_ref,
    out_d_ref,
    out_b_ref,
    out_c_ref,
):
    length = out_b_ref.shape[0]
    first, second = slice(0, length), slice(length, 2 * length)
    heads = slice(2 * length, 2 * length + HEADS)
    out_b_ref[...] = both_ref[first, :]
    out_c_ref[...] = both_ref[second, :]
    state, grad = whole_state(state_ref, 0), whole_state(state_ref, STATE)
    sx, sg = scaled_ref[first, :], scaled_ref[second, :]
    pick = (iota((HEADS, WIDE), 0) == iota((HEADS, WIDE), 1) >> 6).astype(F32)
    whole = jnp.sum(grad.astype(F32) * state.astype(F32), axis=0, keepdims=True) * wide_ref[heads, :]
    whole = jnp.sum(pick * whole, axis=1, keepdims=True)
    from_state = matmul(maps_ref[second, :], state)
    state_back = matmul(maps_ref[first, :], grad)
    out_x_ref[...] = (wide_ref[first, :] + wide_ref[second, :] * state_back).astype(BF16)
    through_head = sum_heads(pick, sg.astype(F32) * from_state)
    through_tail = sum_heads(pick, sx.astype(F32) * state_back)
    one, two = iota((length, length), 0), iota((length, length), 1)
    out_d_ref[...] = (
        narrow_ref[heads, :]
        + matmul(through_head, (one >= two).astype(F32), HIGHEST)
        + matmul(through_tail, (one < two).astype(F32), HIGHEST)
        + whole
    )


def struct(shape, dtype):
    return jax.ShapeDtypeStruct(shape, dtype)


def call(kernel, out, operands, name, specs=None, scratch=(), flops=0, moved=0, limit=24):
    return pl.pallas_call(
        kernel,
        out_shape=out,
        in_specs=specs or [VMEM] * len(operands),
        out_specs=jax.tree.map(lambda _: VMEM, out),
        scratch_shapes=list(scratch),
        cost_estimate=pl.CostEstimate(flops=flops, bytes_accessed=moved, transcendentals=0),
        compiler_params=pltpu.CompilerParams(vmem_limit_bytes=limit * 2**20),
        name=name,
    )(*operands)


def local(inputs, log_decay, b_proj, c_proj, grad_out, w_bc):
    length = inputs.shape[0]
    width = w_bc.shape[2]
    block = [
        pltpu.with_memory_space_constraint(part, pltpu.HBM)
        for part in (log_decay, inputs, grad_out, b_proj, c_proj)
    ]
    held = [pltpu.VMEM(part.shape, part.dtype) for part in block]
    near = call(
        states_kernel,
        struct((LO, NEAR, LANES), BF16),
        block,
        "states",
        specs=[HBM] * 5,
        scratch=held + [pltpu.SemaphoreType.DMA((5,))],
        flops=4 * length * N * WIDE,
        moved=2**20,
    )
    near = lax.all_to_all(near, "lo", 0, 0, axis_index_groups=[NEAR_ORDER])
    far = call(
        segment_kernel,
        struct((HI, FAR, LANES), BF16),
        (near,),
        "segment",
        moved=2**19,
    )
    far = lax.all_to_all(far, "hi", 0, 0, axis_index_groups=[FAR_ORDER])
    inside = call(
        block_kernel,
        (
            struct((2 * length + HEADS, WIDE), F32),
            struct((2 * length + HEADS, N), F32),
            struct((2 * length, WIDE), BF16),
            struct((2 * length, N), BF16),
        ),
        block,
        "block",
        specs=[HBM] * 5,
        scratch=held + [pltpu.SemaphoreType.DMA((5,))],
        flops=2**30,
        moved=4 * 2**20,
    )
    far, inside = lax.optimization_barrier((far, inside))
    states = call(
        entering_kernel,
        struct((LO, 2 * STATE, LANES), BF16),
        (far, near),
        "entering",
        moved=2**19,
    )
    states = lax.all_to_all(states, "lo", 0, 0, axis_index_groups=[BACK_ORDER])
    wide, narrow, scaled, maps = inside
    both, keep, send = call(
        tokens_kernel,
        (
            struct((2 * length, N), BF16),
            struct((length // 2, width), BF16),
            struct((length // 2, width), BF16),
        ),
        (states, narrow, scaled, w_bc.reshape(2 * N, width)),
        "tokens",
        flops=2**29,
        moved=4 * 2**20,
    )
    grad_inputs, grad_decay, grad_b, grad_c = call(
        carried_kernel,
        (
            struct((length, WIDE), BF16),
            struct((HEADS, length), F32),
            struct((length, N), BF16),
            struct((length, N), BF16),
        ),
        (states, wide, narrow, scaled, both, maps),
        "carried",
        flops=2**28,
        moved=2 * 2**20,
    )
    other = lax.ppermute(send, "core", [(0, 1), (1, 0)])
    rest = (grad_inputs, grad_decay, grad_b, grad_c)
    other, (grad_inputs, grad_decay, grad_b, grad_c) = lax.optimization_barrier((other, rest))
    pair = (keep.astype(F32) + other.astype(F32)).astype(BF16)
    blocks = pair.reshape(4, length // 8, width)
    blocks = lax.all_to_all(blocks, "x", 0, 0, axis_index_groups=[X_ORDER])
    grad_tokens = jnp.sum(blocks.astype(F32), axis=0).astype(BF16)
    return grad_inputs, grad_decay, grad_b, grad_c, grad_tokens


def solution(mesh):
    fine = Mesh(mesh.devices.reshape(HI, LO, 4, 2), ("hi", "lo", "x", "core"))
    ctx, head = ("hi", "lo"), ("x", "core")
    return jax.shard_map(
        local,
        mesh=fine,
        in_specs=(P(ctx, head), P(head, ctx), P(ctx, head), P(ctx, head), P(ctx, head), P(None, head, None)),
        out_specs=(P(ctx, head), P(head, ctx), P(ctx, head), P(ctx, head), P(ctx + head, None)),
        check_vma=False,
    )
```

```python
import functools

import jax
import jax.numpy as jnp
from jax import lax
from jax.experimental import pallas as pl
from jax.experimental.pallas import tpu as pltpu
from jax.sharding import Mesh, PartitionSpec as P

F32 = jnp.float32
BF16 = jnp.bfloat16
P_SIZE = 64
N = 128
HEADS = 8
WIDE = HEADS * P_SIZE
LO = 8
HI = 8
LANES = 128
ROWS = N // LO
HIGHEST = lax.Precision.HIGHEST
GROUPS = WIDE // LANES
STATE = GROUPS * ROWS
NEAR = 2 * STATE + 16
FAR = STATE + 16
NEAR_ORDER = [7, 0, 1, 2, 3, 4, 5, 6]
FAR_ORDER = [4, 5, 6, 7, 0, 1, 2, 3]
BACK_ORDER = [6, 7, 0, 1, 2, 3, 4, 5]
X_ORDER = [2, 3, 0, 1]
NEAR_ORDER_OF = [NEAR_ORDER.index(k) for k in range(LO)]
VMEM = pl.BlockSpec(memory_space=pltpu.VMEM)
HBM = pl.BlockSpec(memory_space=pltpu.HBM)


def iota(shape, axis):
    return lax.broadcasted_iota(jnp.int32, shape, axis)


def matmul(a, b, precision=None):
    return lax.dot_general(
        a, b, (((1,), (0,)), ((), ())), precision=precision, preferred_element_type=F32
    )


def matmul_nt(a, b, precision=None):
    return lax.dot_general(
        a, b, (((1,), (1,)), ((), ())), precision=precision, preferred_element_type=F32
    )


def matmul_tn(a, b):
    return lax.dot_general(a, b, (((0,), (0,)), ((), ())), preferred_element_type=F32)


def three_parts(values):
    first = values.astype(BF16).astype(F32)
    rest = values - first
    second = rest.astype(BF16).astype(F32)
    return jnp.concatenate([first, second, rest - second], axis=0).astype(BF16)


def cumulative(rate):
    length = rate.shape[1]
    upper = (iota((length, length), 0) <= iota((length, length), 1)).astype(BF16)
    rows = matmul(three_parts(rate), upper)
    rows = rows[0:HEADS] + rows[HEADS : 2 * HEADS] + rows[2 * HEADS : 3 * HEADS]
    return rows, three_parts(rows)


def widen(parts):
    part, column = iota((3 * HEADS, WIDE + LANES), 0), iota((3 * HEADS, WIDE + LANES), 1)
    of_head = jnp.logical_and((part & 7) == (column >> 6), column < WIDE)
    pick = jnp.logical_or(of_head, column - WIDE == part)
    return matmul_tn(parts, pick.astype(BF16))


def split_three(row):
    lane = iota(row.shape, 1)
    first = row.astype(BF16).astype(F32)
    rest = row - first
    second = rest.astype(BF16).astype(F32)
    third = rest - second
    parts = jnp.where(lane < HEADS, first, jnp.where(lane < 2 * HEADS, second, third))
    return jnp.where(lane < 3 * HEADS, parts, 0.0).astype(BF16)


def join_three(rows):
    lane, column = iota((LANES, WIDE), 0), iota((LANES, WIDE), 1)
    pick = jnp.logical_and((lane & 7) == (column >> 6), lane < 3 * HEADS)
    return matmul(rows, pick.astype(BF16))


def start_copies(sources, targets, sems):
    copies = [
        pltpu.make_async_copy(source, target, sems.at[k])
        for k, (source, target) in enumerate(zip(sources, targets))
    ]
    for copy in copies:
        copy.start()
    return copies


def states_kernel(rate_in, x_in, g_in, b_in, c_in, out_ref, rate_ref, x_ref, g_ref, b_ref, c_ref, sems):
    copies = start_copies(
        (rate_in, x_in, g_in, b_in, c_in), (rate_ref, x_ref, g_ref, b_ref, c_ref), sems
    )
    copies[0].wait()
    _, parts = cumulative(rate_ref[...])
    wide = widen(parts)
    length = wide.shape[0]
    last = wide[length - 1 : length, 0:WIDE]
    total = wide[length - 1 : length, WIDE : WIDE + LANES].astype(BF16)
    total = jnp.broadcast_to(total, (NEAR - 2 * STATE, LANES))
    wide = wide[:, 0:WIDE]
    tail = jnp.exp(last - wide)
    head = jnp.exp(wide)
    for copy in copies[1:]:
        copy.wait()
    scaled_inputs = (x_ref[...].astype(F32) * tail).astype(BF16)
    scaled_grads = (g_ref[...].astype(F32) * head).astype(BF16)
    state = matmul_tn(b_ref[...], scaled_inputs).astype(BF16)
    grad = matmul_tn(c_ref[...], scaled_grads).astype(BF16)
    for place, block in enumerate(NEAR_ORDER):
        rows = slice(block * ROWS, (block + 1) * ROWS)
        for k in range(GROUPS):
            at = slice(k * LANES, (k + 1) * LANES)
            out_ref[place, k * ROWS : (k + 1) * ROWS, :] = state[rows, at]
            out_ref[place, STATE + k * ROWS : STATE + (k + 1) * ROWS, :] = grad[rows, at]
        out_ref[place, 2 * STATE : NEAR, :] = total


def totals_of(ref, row):
    rows = [ref[k, row : row + 16, :].astype(F32)[0:1] for k in range(ref.shape[0])]
    rows = jnp.concatenate(rows, axis=0)
    return rows, join_three(rows.astype(BF16))


def chunk_decays(wide):
    decay = jnp.exp(wide)
    return [
        jnp.concatenate(
            [
                jnp.broadcast_to(decay[k : k + 1, j * LANES : (j + 1) * LANES], (ROWS, LANES))
                for j in range(GROUPS)
            ],
            axis=0,
        )
        for k in range(decay.shape[0])
    ]


def segment_kernel(in_ref, out_ref):
    me = lax.axis_index("hi")
    rows, wide = totals_of(in_ref, 2 * STATE)
    decay = chunk_decays(wide)
    state = jnp.zeros((STATE, LANES), F32)
    grad = jnp.zeros((STATE, LANES), F32)
    for k in NEAR_ORDER_OF:
        state = decay[k] * state + in_ref[k, 0:STATE, :].astype(F32)
    for j in reversed(NEAR_ORDER_OF):
        grad = decay[j] * grad + in_ref[j, STATE : 2 * STATE, :].astype(F32)
    lane, other = iota((LANES, LANES), 0), iota((LANES, LANES), 1)
    fold = jnp.logical_and((lane & 7) == (other & 7), lane < 3 * HEADS).astype(F32)
    total = jnp.sum(matmul(rows, fold, HIGHEST), axis=0, keepdims=True)
    total = jnp.broadcast_to(split_three(total), (FAR - STATE, LANES))
    state = state.astype(BF16)
    grad = grad.astype(BF16)
    for k, segment in enumerate(FAR_ORDER):
        out_ref[k, 0:STATE, :] = jnp.where(segment > me, state, grad)
        out_ref[k, STATE:FAR, :] = total


def entering_kernel(far_ref, near_ref, out_ref):
    me = lax.axis_index("hi")
    far = chunk_decays(totals_of(far_ref, STATE)[1])
    near = chunk_decays(totals_of(near_ref, 2 * STATE)[1])
    state = jnp.zeros((STATE, LANES), F32)
    grad = jnp.zeros((STATE, LANES), F32)
    for k in range(HI):
        at = FAR_ORDER.index(k)
        new = far[at] * state + far_ref[at, 0:STATE, :].astype(F32)
        state = jnp.where(k < me, new, state)
        j = HI - 1 - k
        at = FAR_ORDER.index(j)
        new = far[at] * grad + far_ref[at, 0:STATE, :].astype(F32)
        grad = jnp.where(j > me, new, grad)
    for k in range(LO):
        at = NEAR_ORDER.index(k)
        out_ref[BACK_ORDER.index(k), 0:STATE, :] = state.astype(BF16)
        state = near[at] * state + near_ref[at, 0:STATE, :].astype(F32)
        k = LO - 1 - k
        j = NEAR_ORDER.index(k)
        out_ref[BACK_ORDER.index(k), STATE : 2 * STATE, :] = grad.astype(BF16)
        grad = near[j] * grad + near_ref[j, STATE : 2 * STATE, :].astype(F32)


def block_kernel(
    rate_in,
    x_in,
    g_in,
    b_in,
    c_in,
    wide_ref,
    narrow_ref,
    scaled_ref,
    maps_ref,
    rate_ref,
    x_ref,
    g_ref,
    b_ref,
    c_ref,
    sems,
):
    copies = start_copies(
        (rate_in, x_in, g_in, b_in, c_in), (rate_ref, x_ref, g_ref, b_ref, c_ref), sems
    )
    for copy in copies:
        copy.wait()
    rows, parts = cumulative(rate_ref[...])
    columns = jnp.transpose(rows)
    length = columns.shape[0]
    wide = widen(parts)[:, 0:WIDE]
    last = wide[length - 1 : length]
    tail = jnp.exp(last - wide)
    wide_ref[length : 2 * length, :] = tail
    wide_ref[2 * length : 2 * length + 8, :] = jnp.broadcast_to(jnp.exp(last), (8, WIDE))
    scaled_ref[0:length, :] = (x_ref[...].astype(F32) * tail).astype(BF16)
    scaled_ref[length : 2 * length, :] = (g_ref[...].astype(F32) * jnp.exp(wide)).astype(BF16)
    b, c = b_ref[...], c_ref[...]
    maps_ref[0:length, :] = b
    maps_ref[length : 2 * length, :] = c
    scores = matmul_nt(b, c)
    source, target = iota((length, length), 0), iota((length, length), 1)
    lower = source <= target
    before = source < target
    after = (source >= target).astype(BF16)
    lane = iota((length, LANES), 1)
    grad_scores = jnp.zeros((length, length), F32)
    decay_rows = []
    for pair in range(HEADS // 2):
        at = slice(pair * LANES, (pair + 1) * LANES)
        x_pair, g_pair = x_ref[:, at], g_ref[:, at]
        weights, masked = [], []
        for side in range(2):
            head = 2 * pair + side
            mine = (lane < P_SIZE) if side == 0 else (lane >= P_SIZE)
            x_mine = jnp.where(mine, x_pair, jnp.zeros_like(x_pair))
            g_mine = jnp.where(mine, g_pair, jnp.zeros_like(g_pair))
            gap = rows[head : head + 1, :] - columns[:, head : head + 1]
            decay = jnp.where(lower, jnp.exp(jnp.where(lower, gap, 0.0)), 0.0)
            grad_weights = matmul_nt(x_mine, g_pair)
            weight = scores * decay
            grad_scores = grad_scores + grad_weights * decay
            product = (grad_weights * weight).astype(BF16)
            through = matmul(product, after)
            decay_rows.append(jnp.sum(jnp.where(before, through, 0.0), axis=0, keepdims=True))
            weights.append(weight.astype(BF16))
            masked.append(g_mine)
        wide_ref[0:length, at] = matmul(jnp.concatenate(weights, axis=1), jnp.concatenate(masked, axis=0))
    narrow_ref[2 * length : 2 * length + HEADS, :] = jnp.concatenate(decay_rows, axis=0)
    narrow_ref[0:length, :] = matmul(grad_scores.astype(BF16), c)
    narrow_ref[length : 2 * length, :] = matmul(jnp.transpose(grad_scores).astype(BF16), b)


def whole_state(ref, row):
    parts = []
    for k in range(GROUPS):
        at = slice(row + k * ROWS, row + (k + 1) * ROWS)
        chunks = [ref[BACK_ORDER.index(block), at, :] for block in range(LO)]
        parts.append(jnp.concatenate(chunks, axis=0))
    return jnp.concatenate(parts, axis=1)


def tokens_kernel(state_ref, narrow_ref, scaled_ref, w_ref, both_ref, keep_ref, send_ref):
    length = scaled_ref.shape[0] // 2
    first, second = slice(0, length), slice(length, 2 * length)
    grad_c = matmul_nt(scaled_ref[second, :], whole_state(state_ref, 0))
    grad_b = matmul_nt(scaled_ref[first, :], whole_state(state_ref, STATE))
    grad_c = (grad_c + narrow_ref[second, :]).astype(BF16)
    grad_b = (grad_b + narrow_ref[first, :]).astype(BF16)
    both_ref[first, :] = grad_b
    both_ref[second, :] = grad_c
    both = jnp.concatenate([grad_b, grad_c], axis=1)
    rows = length // 8
    even = jnp.concatenate([both[2 * k * rows : (2 * k + 1) * rows] for k in X_ORDER], axis=0)
    odd = jnp.concatenate([both[(2 * k + 1) * rows : (2 * k + 2) * rows] for k in X_ORDER], axis=0)
    here = lax.axis_index("core") == 0
    keep = jnp.where(here, even, odd)
    send = jnp.where(here, odd, even)
    both = jnp.concatenate([keep, send], axis=0)
    half = length // 2
    step = 512
    for k in range(w_ref.shape[1] // step):
        at = slice(k * step, (k + 1) * step)
        part = matmul(both, w_ref[:, at]).astype(BF16)
        keep_ref[:, at] = part[:half]
        send_ref[:, at] = part[half:]


def sum_heads(pick, values):
    pick = pick.astype(BF16)
    high = values.astype(BF16)
    low = (values - high.astype(F32)).astype(BF16)
    return matmul_nt(pick, high) + matmul_nt(pick, low)


def carried_kernel(
    state_ref,
    wide_ref,
    narrow_ref,
    scaled_ref,
    both_ref,
    maps_ref,
    out_x_ref,
    out_d_ref,
    out_b_ref,
    out_c_ref,
):
    length = out_b_ref.shape[0]
    first, second = slice(0, length), slice(length, 2 * length)
    heads = slice(2 * length, 2 * length + HEADS)
    out_b_ref[...] = both_ref[first, :]
    out_c_ref[...] = both_ref[second, :]
    state, grad = whole_state(state_ref, 0), whole_state(state_ref, STATE)
    sx, sg = scaled_ref[first, :], scaled_ref[second, :]
    pick = (iota((HEADS, WIDE), 0) == iota((HEADS, WIDE), 1) >> 6).astype(F32)
    whole = jnp.sum(grad.astype(F32) * state.astype(F32), axis=0, keepdims=True) * wide_ref[heads, :]
    whole = jnp.sum(pick * whole, axis=1, keepdims=True)
    from_state = matmul(maps_ref[second, :], state)
    state_back = matmul(maps_ref[first, :], grad)
    out_x_ref[...] = (wide_ref[first, :] + wide_ref[second, :] * state_back).astype(BF16)
    through_head = sum_heads(pick, sg.astype(F32) * from_state)
    through_tail = sum_heads(pick, sx.astype(F32) * state_back)
    one, two = iota((length, length), 0), iota((length, length), 1)
    out_d_ref[...] = (
        narrow_ref[heads, :]
        + matmul(through_head, (one >= two).astype(F32), HIGHEST)
        + matmul(through_tail, (one < two).astype(F32), HIGHEST)
        + whole
    )


def struct(shape, dtype):
    return jax.ShapeDtypeStruct(shape, dtype)


def call(kernel, out, operands, name, specs=None, scratch=(), flops=0, moved=0, limit=24):
    return pl.pallas_call(
        kernel,
        out_shape=out,
        in_specs=specs or [VMEM] * len(operands),
        out_specs=jax.tree.map(lambda _: VMEM, out),
        scratch_shapes=list(scratch),
        cost_estimate=pl.CostEstimate(flops=flops, bytes_accessed=moved, transcendentals=0),
        compiler_params=pltpu.CompilerParams(vmem_limit_bytes=limit * 2**20),
        name=name,
    )(*operands)


def local(inputs, log_decay, b_proj, c_proj, grad_out, w_bc):
    length = inputs.shape[0]
    width = w_bc.shape[2]
    block = [
        pltpu.with_memory_space_constraint(part, pltpu.HBM)
        for part in (log_decay, inputs, grad_out, b_proj, c_proj)
    ]
    held = [pltpu.VMEM(part.shape, part.dtype) for part in block]
    near = call(
        states_kernel,
        struct((LO, NEAR, LANES), BF16),
        block,
        "states",
        specs=[HBM] * 5,
        scratch=held + [pltpu.SemaphoreType.DMA((5,))],
        flops=4 * length * N * WIDE,
        moved=2**20,
    )
    near = lax.all_to_all(near, "lo", 0, 0, axis_index_groups=[NEAR_ORDER])
    far = call(
        segment_kernel,
        struct((HI, FAR, LANES), BF16),
        (near,),
        "segment",
        moved=2**19,
    )
    far = lax.all_to_all(far, "hi", 0, 0, axis_index_groups=[FAR_ORDER])
    inside = call(
        block_kernel,
        (
            struct((2 * length + HEADS, WIDE), F32),
            struct((2 * length + HEADS, N), F32),
            struct((2 * length, WIDE), BF16),
            struct((2 * length, N), BF16),
        ),
        block,
        "block",
        specs=[HBM] * 5,
        scratch=held + [pltpu.SemaphoreType.DMA((5,))],
        flops=2**30,
        moved=4 * 2**20,
    )
    far, inside = lax.optimization_barrier((far, inside))
    states = call(
        entering_kernel,
        struct((LO, 2 * STATE, LANES), BF16),
        (far, near),
        "entering",
        moved=2**19,
    )
    states = lax.all_to_all(states, "lo", 0, 0, axis_index_groups=[BACK_ORDER])
    wide, narrow, scaled, maps = inside
    both, keep, send = call(
        tokens_kernel,
        (
            struct((2 * length, N), BF16),
            struct((length // 2, width), BF16),
            struct((length // 2, width), BF16),
        ),
        (states, narrow, scaled, w_bc.reshape(2 * N, width)),
        "tokens",
        flops=2**29,
        moved=4 * 2**20,
    )
    grad_inputs, grad_decay, grad_b, grad_c = call(
        carried_kernel,
        (
            struct((length, WIDE), BF16),
            struct((HEADS, length), F32),
            struct((length, N), BF16),
            struct((length, N), BF16),
        ),
        (states, wide, narrow, scaled, both, maps),
        "carried",
        flops=2**28,
        moved=2 * 2**20,
    )
    other = lax.ppermute(send, "core", [(0, 1), (1, 0)])
    rest = (grad_inputs, grad_decay, grad_b, grad_c)
    other, (grad_inputs, grad_decay, grad_b, grad_c) = lax.optimization_barrier((other, rest))
    pair = (keep.astype(F32) + other.astype(F32)).astype(BF16)
    blocks = pair.reshape(4, length // 8, width)
    blocks = lax.all_to_all(blocks, "x", 0, 0, axis_index_groups=[X_ORDER])
    grad_tokens = jnp.sum(blocks.astype(F32), axis=0).astype(BF16)
    return grad_inputs, grad_decay, grad_b, grad_c, grad_tokens


def solution(mesh):
    fine = Mesh(mesh.devices.reshape(HI, LO, 4, 2), ("hi", "lo", "x", "core"))
    ctx, head = ("hi", "lo"), ("x", "core")
    return jax.shard_map(
        local,
        mesh=fine,
        in_specs=(P(ctx, head), P(head, ctx), P(ctx, head), P(ctx, head), P(ctx, head), P(None, head, None)),
        out_specs=(P(ctx, head), P(head, ctx), P(ctx, head), P(ctx, head), P(ctx + head, None)),
        check_vma=False,
    )
```

```python
import functools

import jax
import jax.numpy as jnp
from jax import lax
from jax.experimental import pallas as pl
from jax.experimental.pallas import tpu as pltpu
from jax.sharding import Mesh, PartitionSpec as P

F32 = jnp.float32
BF16 = jnp.bfloat16
P_SIZE = 64
N = 128
HEADS = 8
WIDE = HEADS * P_SIZE
LO = 8
HI = 8
LANES = 128
ROWS = N // LO
HIGHEST = lax.Precision.HIGHEST
GROUPS = WIDE // LANES
STATE = GROUPS * ROWS
NEAR = 2 * STATE + 16
FAR = STATE + 16
EARLY = 3
NEAR_ORDER = [7, 6, 5, 4, 3, 2, 1, 0]
FAR_ORDER = [4, 5, 6, 7, 0, 1, 2, 3]
BACK_ORDER = [6, 7, 0, 1, 2, 3, 4, 5]
X_ORDER = [2, 3, 0, 1]
NEAR_ORDER_OF = [NEAR_ORDER.index(k) for k in range(LO)]
VMEM = pl.BlockSpec(memory_space=pltpu.VMEM)
HBM = pl.BlockSpec(memory_space=pltpu.HBM)


def iota(shape, axis):
    return lax.broadcasted_iota(jnp.int32, shape, axis)


def matmul(a, b, precision=None):
    return lax.dot_general(
        a, b, (((1,), (0,)), ((), ())), precision=precision, preferred_element_type=F32
    )


def matmul_nt(a, b, precision=None):
    return lax.dot_general(
        a, b, (((1,), (1,)), ((), ())), precision=precision, preferred_element_type=F32
    )


def matmul_tn(a, b):
    return lax.dot_general(a, b, (((0,), (0,)), ((), ())), preferred_element_type=F32)


def three_parts(values):
    first = values.astype(BF16).astype(F32)
    rest = values - first
    second = rest.astype(BF16).astype(F32)
    return jnp.concatenate([first, second, rest - second], axis=0).astype(BF16)


def cumulative(rate):
    length = rate.shape[1]
    upper = (iota((length, length), 0) <= iota((length, length), 1)).astype(BF16)
    rows = matmul(three_parts(rate), upper)
    rows = rows[0:HEADS] + rows[HEADS : 2 * HEADS] + rows[2 * HEADS : 3 * HEADS]
    return rows, three_parts(rows)


def widen(parts):
    part, column = iota((3 * HEADS, WIDE + LANES), 0), iota((3 * HEADS, WIDE + LANES), 1)
    of_head = jnp.logical_and((part & 7) == (column >> 6), column < WIDE)
    pick = jnp.logical_or(of_head, column - WIDE == part)
    return matmul_tn(parts, pick.astype(BF16))


def split_three(row):
    lane = iota(row.shape, 1)
    first = row.astype(BF16).astype(F32)
    rest = row - first
    second = rest.astype(BF16).astype(F32)
    third = rest - second
    parts = jnp.where(lane < HEADS, first, jnp.where(lane < 2 * HEADS, second, third))
    return jnp.where(lane < 3 * HEADS, parts, 0.0).astype(BF16)


def join_three(rows):
    lane, column = iota((LANES, WIDE), 0), iota((LANES, WIDE), 1)
    pick = jnp.logical_and((lane & 7) == (column >> 6), lane < 3 * HEADS)
    return matmul(rows, pick.astype(BF16))


def start_copies(sources, targets, sems):
    copies = [
        pltpu.make_async_copy(source, target, sems.at[k])
        for k, (source, target) in enumerate(zip(sources, targets))
    ]
    for copy in copies:
        copy.start()
    return copies


def states_kernel(rate_in, x_in, g_in, b_in, c_in, out_ref, rate_ref, x_ref, g_ref, b_ref, c_ref, sems):
    copies = start_copies(
        (rate_in, x_in, g_in, b_in, c_in), (rate_ref, x_ref, g_ref, b_ref, c_ref), sems
    )
    copies[0].wait()
    _, parts = cumulative(rate_ref[...])
    wide = widen(parts)
    length = wide.shape[0]
    last = wide[length - 1 : length, 0:WIDE]
    total = wide[length - 1 : length, WIDE : WIDE + LANES].astype(BF16)
    total = jnp.broadcast_to(total, (NEAR - 2 * STATE, LANES))
    wide = wide[:, 0:WIDE]
    tail = jnp.exp(last - wide)
    head = jnp.exp(wide)
    for copy in copies[1:]:
        copy.wait()
    scaled_inputs = (x_ref[...].astype(F32) * tail).astype(BF16)
    scaled_grads = (g_ref[...].astype(F32) * head).astype(BF16)
    state = matmul_tn(b_ref[...], scaled_inputs).astype(BF16)
    grad = matmul_tn(c_ref[...], scaled_grads).astype(BF16)
    for place, block in enumerate(NEAR_ORDER):
        rows = slice(block * ROWS, (block + 1) * ROWS)
        for k in range(GROUPS):
            at = slice(k * LANES, (k + 1) * LANES)
            out_ref[place, k * ROWS : (k + 1) * ROWS, :] = state[rows, at]
            out_ref[place, STATE + k * ROWS : STATE + (k + 1) * ROWS, :] = grad[rows, at]
        out_ref[place, 2 * STATE : NEAR, :] = total


def totals_of(ref, row):
    rows = [ref[k, row : row + 16, :].astype(F32)[0:1] for k in range(ref.shape[0])]
    rows = jnp.concatenate(rows, axis=0)
    return rows, join_three(rows.astype(BF16))


def chunk_decays(wide):
    decay = jnp.exp(wide)
    return [
        jnp.concatenate(
            [
                jnp.broadcast_to(decay[k : k + 1, j * LANES : (j + 1) * LANES], (ROWS, LANES))
                for j in range(GROUPS)
            ],
            axis=0,
        )
        for k in range(decay.shape[0])
    ]


def block_body(
    rate_in,
    x_in,
    g_in,
    b_in,
    c_in,
    wide_ref,
    narrow_ref,
    scaled_ref,
    maps_ref,
    rate_ref,
    x_ref,
    g_ref,
    b_ref,
    c_ref,
    sems,
):
    copies = start_copies(
        (rate_in, x_in, g_in, b_in, c_in), (rate_ref, x_ref, g_ref, b_ref, c_ref), sems
    )
    for copy in copies:
        copy.wait()
    rows, parts = cumulative(rate_ref[...])
    columns = jnp.transpose(rows)
    length = columns.shape[0]
    wide = widen(parts)[:, 0:WIDE]
    last = wide[length - 1 : length]
    tail = jnp.exp(last - wide)
    wide_ref[length : 2 * length, :] = tail
    wide_ref[2 * length : 2 * length + 8, :] = jnp.broadcast_to(jnp.exp(last), (8, WIDE))
    scaled_ref[0:length, :] = (x_ref[...].astype(F32) * tail).astype(BF16)
    scaled_ref[length : 2 * length, :] = (g_ref[...].astype(F32) * jnp.exp(wide)).astype(BF16)
    b, c = b_ref[...], c_ref[...]
    maps_ref[0:length, :] = b
    maps_ref[length : 2 * length, :] = c
    scores = matmul_nt(b, c)
    source, target = iota((length, length), 0), iota((length, length), 1)
    lower = source <= target
    before = source < target
    after = (source >= target).astype(BF16)
    lane = iota((length, LANES), 1)
    grad_scores = jnp.zeros((length, length), F32)
    decay_rows = []
    for pair in range(HEADS // 2):
        at = slice(pair * LANES, (pair + 1) * LANES)
        x_pair, g_pair = x_ref[:, at], g_ref[:, at]
        weights, masked = [], []
        for side in range(2):
            head = 2 * pair + side
            mine = (lane < P_SIZE) if side == 0 else (lane >= P_SIZE)
            x_mine = jnp.where(mine, x_pair, jnp.zeros_like(x_pair))
            g_mine = jnp.where(mine, g_pair, jnp.zeros_like(g_pair))
            gap = rows[head : head + 1, :] - columns[:, head : head + 1]
            decay = jnp.where(lower, jnp.exp(jnp.where(lower, gap, 0.0)), 0.0)
            grad_weights = matmul_nt(x_mine, g_pair)
            weight = scores * decay
            grad_scores = grad_scores + grad_weights * decay
            product = (grad_weights * weight).astype(BF16)
            through = matmul(product, after)
            decay_rows.append(jnp.sum(jnp.where(before, through, 0.0), axis=0, keepdims=True))
            weights.append(weight.astype(BF16))
            masked.append(g_mine)
        wide_ref[0:length, at] = matmul(jnp.concatenate(weights, axis=1), jnp.concatenate(masked, axis=0))
    narrow_ref[2 * length : 2 * length + HEADS, :] = jnp.concatenate(decay_rows, axis=0)
    narrow_ref[0:length, :] = matmul(grad_scores.astype(BF16), c)
    narrow_ref[length : 2 * length, :] = matmul(jnp.transpose(grad_scores).astype(BF16), b)


def segment_kernel(in_ref, rate_in, x_in, g_in, b_in, c_in, out_ref, *rest):
    me = lax.axis_index("hi")
    rows, wide = totals_of(in_ref, 2 * STATE)
    decay = chunk_decays(wide)
    state = jnp.zeros((STATE, LANES), F32)
    grad = jnp.zeros((STATE, LANES), F32)
    for k in NEAR_ORDER_OF:
        state = decay[k] * state + in_ref[k, 0:STATE, :].astype(F32)
    for j in reversed(NEAR_ORDER_OF):
        grad = decay[j] * grad + in_ref[j, STATE : 2 * STATE, :].astype(F32)
    lane, other = iota((LANES, LANES), 0), iota((LANES, LANES), 1)
    fold = jnp.logical_and((lane & 7) == (other & 7), lane < 3 * HEADS).astype(F32)
    total = jnp.sum(matmul(rows, fold, HIGHEST), axis=0, keepdims=True)
    total = jnp.broadcast_to(split_three(total), (FAR - STATE, LANES))
    state = state.astype(BF16)
    grad = grad.astype(BF16)
    for k, segment in enumerate(FAR_ORDER):
        out_ref[k, 0:STATE, :] = jnp.where(segment > me, state, grad)
        out_ref[k, STATE:FAR, :] = total

    @pl.when(me < EARLY)
    def _():
        block_body(rate_in, x_in, g_in, b_in, c_in, *rest)


def entering_kernel(far_ref, near_ref, rate_in, x_in, g_in, b_in, c_in, out_ref, *rest):
    me = lax.axis_index("hi")
    far = chunk_decays(totals_of(far_ref, STATE)[1])
    near = chunk_decays(totals_of(near_ref, 2 * STATE)[1])
    state = jnp.zeros((STATE, LANES), F32)
    grad = jnp.zeros((STATE, LANES), F32)
    for k in range(HI):
        at = FAR_ORDER.index(k)
        new = far[at] * state + far_ref[at, 0:STATE, :].astype(F32)
        state = jnp.where(k < me, new, state)
        j = HI - 1 - k
        at = FAR_ORDER.index(j)
        new = far[at] * grad + far_ref[at, 0:STATE, :].astype(F32)
        grad = jnp.where(j > me, new, grad)
    for k in range(LO):
        at = NEAR_ORDER.index(k)
        out_ref[BACK_ORDER.index(k), 0:STATE, :] = state.astype(BF16)
        state = near[at] * state + near_ref[at, 0:STATE, :].astype(F32)
        k = LO - 1 - k
        j = NEAR_ORDER.index(k)
        out_ref[BACK_ORDER.index(k), STATE : 2 * STATE, :] = grad.astype(BF16)
        grad = near[j] * grad + near_ref[j, STATE : 2 * STATE, :].astype(F32)

    @pl.when(me >= EARLY)
    def _():
        block_body(rate_in, x_in, g_in, b_in, c_in, *rest)


def whole_state(ref, row):
    parts = []
    for k in range(GROUPS):
        at = slice(row + k * ROWS, row + (k + 1) * ROWS)
        chunks = [ref[BACK_ORDER.index(block), at, :] for block in range(LO)]
        parts.append(jnp.concatenate(chunks, axis=0))
    return jnp.concatenate(parts, axis=1)


def either(pair, at):
    return jnp.where(lax.axis_index("hi") < EARLY, pair[0][at, :], pair[1][at, :])


def tokens_kernel(state_ref, narrow_a, scaled_a, narrow_b, scaled_b, w_ref, both_ref, keep_ref, send_ref):
    narrow, scaled = (narrow_a, narrow_b), (scaled_a, scaled_b)
    length = scaled_a.shape[0] // 2
    first, second = slice(0, length), slice(length, 2 * length)
    grad_c = matmul_nt(either(scaled, second), whole_state(state_ref, 0))
    grad_b = matmul_nt(either(scaled, first), whole_state(state_ref, STATE))
    grad_c = (grad_c + either(narrow, second)).astype(BF16)
    grad_b = (grad_b + either(narrow, first)).astype(BF16)
    both_ref[first, :] = grad_b
    both_ref[second, :] = grad_c
    both = jnp.concatenate([grad_b, grad_c], axis=1)
    rows = length // 8
    even = jnp.concatenate([both[2 * k * rows : (2 * k + 1) * rows] for k in X_ORDER], axis=0)
    odd = jnp.concatenate([both[(2 * k + 1) * rows : (2 * k + 2) * rows] for k in X_ORDER], axis=0)
    here = lax.axis_index("core") == 0
    keep = jnp.where(here, even, odd)
    send = jnp.where(here, odd, even)
    both = jnp.concatenate([keep, send], axis=0)
    half = length // 2
    step = 512
    for k in range(w_ref.shape[1] // step):
        at = slice(k * step, (k + 1) * step)
        part = matmul(both, w_ref[:, at]).astype(BF16)
        keep_ref[:, at] = part[:half]
        send_ref[:, at] = part[half:]


def sum_heads(pick, values):
    pick = pick.astype(BF16)
    high = values.astype(BF16)
    low = (values - high.astype(F32)).astype(BF16)
    return matmul_nt(pick, high) + matmul_nt(pick, low)


def carried_kernel(
    state_ref,
    both_ref,
    wide_a,
    narrow_a,
    scaled_a,
    maps_a,
    wide_b,
    narrow_b,
    scaled_b,
    maps_b,
    out_x_ref,
    out_d_ref,
    out_b_ref,
    out_c_ref,
):
    wide, narrow = (wide_a, wide_b), (narrow_a, narrow_b)
    scaled, maps = (scaled_a, scaled_b), (maps_a, maps_b)
    length = out_b_ref.shape[0]
    first, second = slice(0, length), slice(length, 2 * length)
    heads = slice(2 * length, 2 * length + HEADS)
    out_b_ref[...] = both_ref[first, :]
    out_c_ref[...] = both_ref[second, :]
    state, grad = whole_state(state_ref, 0), whole_state(state_ref, STATE)
    sx, sg = either(scaled, first), either(scaled, second)
    pick = (iota((HEADS, WIDE), 0) == iota((HEADS, WIDE), 1) >> 6).astype(F32)
    whole = jnp.sum(grad.astype(F32) * state.astype(F32), axis=0, keepdims=True) * either(wide, heads)
    whole = jnp.sum(pick * whole, axis=1, keepdims=True)
    from_state = matmul(either(maps, second), state)
    state_back = matmul(either(maps, first), grad)
    out_x_ref[...] = (either(wide, first) + either(wide, second) * state_back).astype(BF16)
    through_head = sum_heads(pick, sg.astype(F32) * from_state)
    through_tail = sum_heads(pick, sx.astype(F32) * state_back)
    one, two = iota((length, length), 0), iota((length, length), 1)
    out_d_ref[...] = (
        either(narrow, heads)
        + matmul(through_head, (one >= two).astype(F32), HIGHEST)
        + matmul(through_tail, (one < two).astype(F32), HIGHEST)
        + whole
    )


def struct(shape, dtype):
    return jax.ShapeDtypeStruct(shape, dtype)


def call(kernel, out, operands, name, specs=None, scratch=(), flops=0, moved=0, limit=24):
    return pl.pallas_call(
        kernel,
        out_shape=out,
        in_specs=specs or [VMEM] * len(operands),
        out_specs=jax.tree.map(lambda _: VMEM, out),
        scratch_shapes=list(scratch),
        cost_estimate=pl.CostEstimate(flops=flops, bytes_accessed=moved, transcendentals=0),
        compiler_params=pltpu.CompilerParams(vmem_limit_bytes=limit * 2**20),
        name=name,
    )(*operands)


def local(inputs, log_decay, b_proj, c_proj, grad_out, w_bc):
    length = inputs.shape[0]
    width = w_bc.shape[2]
    block = [
        pltpu.with_memory_space_constraint(part, pltpu.HBM)
        for part in (log_decay, inputs, grad_out, b_proj, c_proj)
    ]
    held = [pltpu.VMEM(part.shape, part.dtype) for part in block]
    near = call(
        states_kernel,
        struct((LO, NEAR, LANES), BF16),
        block,
        "states",
        specs=[HBM] * 5,
        scratch=held + [pltpu.SemaphoreType.DMA((5,))],
        flops=4 * length * N * WIDE,
        moved=2**20,
    )
    near = lax.all_to_all(near, "lo", 0, 0, axis_index_groups=[NEAR_ORDER])
    inside = (
        struct((2 * length + HEADS, WIDE), F32),
        struct((2 * length + HEADS, N), F32),
        struct((2 * length, WIDE), BF16),
        struct((2 * length, N), BF16),
    )
    scratch = held + [pltpu.SemaphoreType.DMA((5,))]
    far, *before = call(
        segment_kernel,
        (struct((HI, FAR, LANES), BF16),) + inside,
        [near] + block,
        "segment",
        specs=[VMEM] + [HBM] * 5,
        scratch=scratch,
        moved=2**19,
    )
    far = lax.all_to_all(far, "hi", 0, 0, axis_index_groups=[FAR_ORDER])
    states, *after = call(
        entering_kernel,
        (struct((LO, 2 * STATE, LANES), BF16),) + inside,
        [far, near] + block,
        "entering",
        specs=[VMEM] * 2 + [HBM] * 5,
        scratch=scratch,
        moved=2**19,
    )
    states = lax.all_to_all(states, "lo", 0, 0, axis_index_groups=[BACK_ORDER])
    both, keep, send = call(
        tokens_kernel,
        (
            struct((2 * length, N), BF16),
            struct((length // 2, width), BF16),
            struct((length // 2, width), BF16),
        ),
        (states, before[1], before[2], after[1], after[2], w_bc.reshape(2 * N, width)),
        "tokens",
        flops=2**29,
        moved=4 * 2**20,
    )
    grad_inputs, grad_decay, grad_b, grad_c = call(
        carried_kernel,
        (
            struct((length, WIDE), BF16),
            struct((HEADS, length), F32),
            struct((length, N), BF16),
            struct((length, N), BF16),
        ),
        (states, both, *before, *after),
        "carried",
        flops=2**28,
        moved=2 * 2**20,
    )
    other = lax.ppermute(send, "core", [(0, 1), (1, 0)])
    rest = (grad_inputs, grad_decay, grad_b, grad_c)
    other, (grad_inputs, grad_decay, grad_b, grad_c) = lax.optimization_barrier((other, rest))
    pair = (keep.astype(F32) + other.astype(F32)).astype(BF16)
    blocks = pair.reshape(4, length // 8, width)
    blocks = lax.all_to_all(blocks, "x", 0, 0, axis_index_groups=[X_ORDER])
    grad_tokens = jnp.sum(blocks.astype(F32), axis=0).astype(BF16)
    return grad_inputs, grad_decay, grad_b, grad_c, grad_tokens


def solution(mesh):
    fine = Mesh(mesh.devices.reshape(HI, LO, 4, 2), ("hi", "lo", "x", "core"))
    ctx, head = ("hi", "lo"), ("x", "core")
    return jax.shard_map(
        local,
        mesh=fine,
        in_specs=(P(ctx, head), P(head, ctx), P(ctx, head), P(ctx, head), P(ctx, head), P(None, head, None)),
        out_specs=(P(ctx, head), P(head, ctx), P(ctx, head), P(ctx, head), P(ctx + head, None)),
        check_vma=False,
    )
```

```python
import functools

import jax
import jax.numpy as jnp
from jax import lax
from jax.experimental import pallas as pl
from jax.experimental.pallas import tpu as pltpu
from jax.sharding import Mesh, PartitionSpec as P

F32 = jnp.float32
BF16 = jnp.bfloat16
P_SIZE = 64
N = 128
HEADS = 8
WIDE = HEADS * P_SIZE
LO = 8
HI = 8
LANES = 128
ROWS = N // LO
HIGHEST = lax.Precision.HIGHEST
GROUPS = WIDE // LANES
STATE = GROUPS * ROWS
NEAR = 2 * STATE + 16
FAR = STATE + 8
EARLY = 3
NEAR_ORDER = [7, 6, 5, 4, 3, 2, 1, 0]
FAR_ORDER = [4, 5, 6, 7, 0, 1, 2, 3]
BACK_ORDER = [6, 7, 0, 1, 2, 3, 4, 5]
X_ORDER = [2, 3, 0, 1]
NEAR_ORDER_OF = [NEAR_ORDER.index(k) for k in range(LO)]
VMEM = pl.BlockSpec(memory_space=pltpu.VMEM)
HBM = pl.BlockSpec(memory_space=pltpu.HBM)


def iota(shape, axis):
    return lax.broadcasted_iota(jnp.int32, shape, axis)


def matmul(a, b, precision=None):
    return lax.dot_general(
        a, b, (((1,), (0,)), ((), ())), precision=precision, preferred_element_type=F32
    )


def matmul_nt(a, b, precision=None):
    return lax.dot_general(
        a, b, (((1,), (1,)), ((), ())), precision=precision, preferred_element_type=F32
    )


def matmul_tn(a, b):
    return lax.dot_general(a, b, (((0,), (0,)), ((), ())), preferred_element_type=F32)


def three_parts(values):
    first = values.astype(BF16).astype(F32)
    rest = values - first
    second = rest.astype(BF16).astype(F32)
    return jnp.concatenate([first, second, rest - second], axis=0).astype(BF16)


def cumulative(rate):
    length = rate.shape[1]
    upper = (iota((length, length), 0) <= iota((length, length), 1)).astype(BF16)
    rows = matmul(three_parts(rate), upper)
    rows = rows[0:HEADS] + rows[HEADS : 2 * HEADS] + rows[2 * HEADS : 3 * HEADS]
    return rows, three_parts(rows)


def widen(parts):
    part, column = iota((3 * HEADS, WIDE + LANES), 0), iota((3 * HEADS, WIDE + LANES), 1)
    of_head = jnp.logical_and((part & 7) == (column >> 6), column < WIDE)
    pick = jnp.logical_or(of_head, column - WIDE == part)
    return matmul_tn(parts, pick.astype(BF16))


def split_three(row):
    lane = iota(row.shape, 1)
    first = row.astype(BF16).astype(F32)
    rest = row - first
    second = rest.astype(BF16).astype(F32)
    third = rest - second
    parts = jnp.where(lane < HEADS, first, jnp.where(lane < 2 * HEADS, second, third))
    return jnp.where(lane < 3 * HEADS, parts, 0.0).astype(BF16)


def join_three(rows):
    lane, column = iota((LANES, WIDE), 0), iota((LANES, WIDE), 1)
    pick = jnp.logical_and((lane & 7) == (column >> 6), lane < 3 * HEADS)
    return matmul(rows, pick.astype(BF16))


def start_copies(sources, targets, sems):
    copies = [
        pltpu.make_async_copy(source, target, sems.at[k])
        for k, (source, target) in enumerate(zip(sources, targets))
    ]
    for copy in copies:
        copy.start()
    return copies


def states_kernel(rate_in, x_in, g_in, b_in, c_in, out_ref, rate_ref, x_ref, g_ref, b_ref, c_ref, sems):
    copies = start_copies(
        (rate_in, x_in, g_in, b_in, c_in), (rate_ref, x_ref, g_ref, b_ref, c_ref), sems
    )
    copies[0].wait()
    _, parts = cumulative(rate_ref[...])
    wide = widen(parts)
    length = wide.shape[0]
    last = wide[length - 1 : length, 0:WIDE]
    total = wide[length - 1 : length, WIDE : WIDE + LANES].astype(BF16)
    total = jnp.broadcast_to(total, (NEAR - 2 * STATE, LANES))
    wide = wide[:, 0:WIDE]
    tail = jnp.exp(last - wide)
    head = jnp.exp(wide)
    for copy in copies[1:]:
        copy.wait()
    scaled_inputs = (x_ref[...].astype(F32) * tail).astype(BF16)
    scaled_grads = (g_ref[...].astype(F32) * head).astype(BF16)
    state = matmul_tn(b_ref[...], scaled_inputs).astype(BF16)
    grad = matmul_tn(c_ref[...], scaled_grads).astype(BF16)
    for place, block in enumerate(NEAR_ORDER):
        rows = slice(block * ROWS, (block + 1) * ROWS)
        for k in range(GROUPS):
            at = slice(k * LANES, (k + 1) * LANES)
            out_ref[place, k * ROWS : (k + 1) * ROWS, :] = state[rows, at]
            out_ref[place, STATE + k * ROWS : STATE + (k + 1) * ROWS, :] = grad[rows, at]
        out_ref[place, 2 * STATE : NEAR, :] = total


def totals_of(ref, row):
    rows = [ref[k, row : ref.shape[1], :].astype(F32)[0:1] for k in range(ref.shape[0])]
    rows = jnp.concatenate(rows, axis=0)
    return rows, join_three(rows.astype(BF16))


def chunk_decays(wide):
    decay = jnp.exp(wide)
    return [
        jnp.concatenate(
            [
                jnp.broadcast_to(decay[k : k + 1, j * LANES : (j + 1) * LANES], (ROWS, LANES))
                for j in range(GROUPS)
            ],
            axis=0,
        )
        for k in range(decay.shape[0])
    ]


def block_body(
    rate_in,
    x_in,
    g_in,
    b_in,
    c_in,
    wide_ref,
    narrow_ref,
    scaled_ref,
    maps_ref,
    rate_ref,
    x_ref,
    g_ref,
    b_ref,
    c_ref,
    sems,
):
    copies = start_copies(
        (rate_in, x_in, g_in, b_in, c_in), (rate_ref, x_ref, g_ref, b_ref, c_ref), sems
    )
    for copy in copies:
        copy.wait()
    rows, parts = cumulative(rate_ref[...])
    columns = jnp.transpose(rows)
    length = columns.shape[0]
    wide = widen(parts)[:, 0:WIDE]
    last = wide[length - 1 : length]
    tail = jnp.exp(last - wide)
    wide_ref[length : 2 * length, :] = tail
    wide_ref[2 * length : 2 * length + 8, :] = jnp.broadcast_to(jnp.exp(last), (8, WIDE))
    scaled_ref[0:length, :] = (x_ref[...].astype(F32) * tail).astype(BF16)
    scaled_ref[length : 2 * length, :] = (g_ref[...].astype(F32) * jnp.exp(wide)).astype(BF16)
    b, c = b_ref[...], c_ref[...]
    maps_ref[0:length, :] = b
    maps_ref[length : 2 * length, :] = c
    scores = matmul_nt(b, c)
    source, target = iota((length, length), 0), iota((length, length), 1)
    lower = source <= target
    before = source < target
    after = (source >= target).astype(BF16)
    lane = iota((length, LANES), 1)
    grad_scores = jnp.zeros((length, length), F32)
    decay_rows = []
    for pair in range(HEADS // 2):
        at = slice(pair * LANES, (pair + 1) * LANES)
        x_pair, g_pair = x_ref[:, at], g_ref[:, at]
        weights, masked = [], []
        for side in range(2):
            head = 2 * pair + side
            mine = (lane < P_SIZE) if side == 0 else (lane >= P_SIZE)
            x_mine = jnp.where(mine, x_pair, jnp.zeros_like(x_pair))
            g_mine = jnp.where(mine, g_pair, jnp.zeros_like(g_pair))
            gap = rows[head : head + 1, :] - columns[:, head : head + 1]
            decay = jnp.where(lower, jnp.exp(jnp.where(lower, gap, 0.0)), 0.0)
            grad_weights = matmul_nt(x_mine, g_pair)
            weight = scores * decay
            grad_scores = grad_scores + grad_weights * decay
            product = (grad_weights * weight).astype(BF16)
            through = matmul(product, after)
            decay_rows.append(jnp.sum(jnp.where(before, through, 0.0), axis=0, keepdims=True))
            weights.append(weight.astype(BF16))
            masked.append(g_mine)
        wide_ref[0:length, at] = matmul(jnp.concatenate(weights, axis=1), jnp.concatenate(masked, axis=0))
    narrow_ref[2 * length : 2 * length + HEADS, :] = jnp.concatenate(decay_rows, axis=0)
    narrow_ref[0:length, :] = matmul(grad_scores.astype(BF16), c)
    narrow_ref[length : 2 * length, :] = matmul(jnp.transpose(grad_scores).astype(BF16), b)


def segment_kernel(in_ref, rate_in, x_in, g_in, b_in, c_in, out_ref, *rest):
    me = lax.axis_index("hi")
    rows, wide = totals_of(in_ref, 2 * STATE)
    decay = chunk_decays(wide)
    state = jnp.zeros((STATE, LANES), F32)
    grad = jnp.zeros((STATE, LANES), F32)
    for k in NEAR_ORDER_OF:
        state = decay[k] * state + in_ref[k, 0:STATE, :].astype(F32)
    for j in reversed(NEAR_ORDER_OF):
        grad = decay[j] * grad + in_ref[j, STATE : 2 * STATE, :].astype(F32)
    lane, other = iota((LANES, LANES), 0), iota((LANES, LANES), 1)
    fold = jnp.logical_and((lane & 7) == (other & 7), lane < 3 * HEADS).astype(F32)
    total = jnp.sum(matmul(rows, fold, HIGHEST), axis=0, keepdims=True)
    total = jnp.broadcast_to(split_three(total), (FAR - STATE, LANES))
    state = state.astype(BF16)
    grad = grad.astype(BF16)
    for k, segment in enumerate(FAR_ORDER):
        out_ref[k, 0:STATE, :] = jnp.where(segment > me, state, grad)
        out_ref[k, STATE:FAR, :] = total

    @pl.when(me < EARLY)
    def _():
        block_body(rate_in, x_in, g_in, b_in, c_in, *rest)


def entering_kernel(far_ref, near_ref, rate_in, x_in, g_in, b_in, c_in, out_ref, *rest):
    me = lax.axis_index("hi")
    far = chunk_decays(totals_of(far_ref, STATE)[1])
    near = chunk_decays(totals_of(near_ref, 2 * STATE)[1])
    state = jnp.zeros((STATE, LANES), F32)
    grad = jnp.zeros((STATE, LANES), F32)
    for k in range(HI):
        at = FAR_ORDER.index(k)
        new = far[at] * state + far_ref[at, 0:STATE, :].astype(F32)
        state = jnp.where(k < me, new, state)
        j = HI - 1 - k
        at = FAR_ORDER.index(j)
        new = far[at] * grad + far_ref[at, 0:STATE, :].astype(F32)
        grad = jnp.where(j > me, new, grad)
    for k in range(LO):
        at = NEAR_ORDER.index(k)
        out_ref[BACK_ORDER.index(k), 0:STATE, :] = state.astype(BF16)
        state = near[at] * state + near_ref[at, 0:STATE, :].astype(F32)
        k = LO - 1 - k
        j = NEAR_ORDER.index(k)
        out_ref[BACK_ORDER.index(k), STATE : 2 * STATE, :] = grad.astype(BF16)
        grad = near[j] * grad + near_ref[j, STATE : 2 * STATE, :].astype(F32)

    @pl.when(me >= EARLY)
    def _():
        block_body(rate_in, x_in, g_in, b_in, c_in, *rest)


def whole_state(ref, row):
    parts = []
    for k in range(GROUPS):
        at = slice(row + k * ROWS, row + (k + 1) * ROWS)
        chunks = [ref[BACK_ORDER.index(block), at, :] for block in range(LO)]
        parts.append(jnp.concatenate(chunks, axis=0))
    return jnp.concatenate(parts, axis=1)


def either(pair, at):
    return jnp.where(lax.axis_index("hi") < EARLY, pair[0][at, :], pair[1][at, :])


def tokens_kernel(state_ref, narrow_a, scaled_a, narrow_b, scaled_b, w_ref, both_ref, keep_ref, send_ref):
    narrow, scaled = (narrow_a, narrow_b), (scaled_a, scaled_b)
    length = scaled_a.shape[0] // 2
    first, second = slice(0, length), slice(length, 2 * length)
    grad_c = matmul_nt(either(scaled, second), whole_state(state_ref, 0))
    grad_b = matmul_nt(either(scaled, first), whole_state(state_ref, STATE))
    grad_c = (grad_c + either(narrow, second)).astype(BF16)
    grad_b = (grad_b + either(narrow, first)).astype(BF16)
    both_ref[first, :] = grad_b
    both_ref[second, :] = grad_c
    both = jnp.concatenate([grad_b, grad_c], axis=1)
    rows = length // 8
    even = jnp.concatenate([both[2 * k * rows : (2 * k + 1) * rows] for k in X_ORDER], axis=0)
    odd = jnp.concatenate([both[(2 * k + 1) * rows : (2 * k + 2) * rows] for k in X_ORDER], axis=0)
    here = lax.axis_index("core") == 0
    keep = jnp.where(here, even, odd)
    send = jnp.where(here, odd, even)
    both = jnp.concatenate([keep, send], axis=0)
    half = length // 2
    step = 512
    for k in range(w_ref.shape[1] // step):
        at = slice(k * step, (k + 1) * step)
        part = matmul(both, w_ref[:, at]).astype(BF16)
        keep_ref[:, at] = part[:half]
        send_ref[:, at] = part[half:]


def sum_heads(pick, values):
    pick = pick.astype(BF16)
    high = values.astype(BF16)
    low = (values - high.astype(F32)).astype(BF16)
    return matmul_nt(pick, high) + matmul_nt(pick, low)


def carried_kernel(
    state_ref,
    both_ref,
    wide_a,
    narrow_a,
    scaled_a,
    maps_a,
    wide_b,
    narrow_b,
    scaled_b,
    maps_b,
    out_x_ref,
    out_d_ref,
    out_b_ref,
    out_c_ref,
):
    wide, narrow = (wide_a, wide_b), (narrow_a, narrow_b)
    scaled, maps = (scaled_a, scaled_b), (maps_a, maps_b)
    length = out_b_ref.shape[0]
    first, second = slice(0, length), slice(length, 2 * length)
    heads = slice(2 * length, 2 * length + HEADS)
    out_b_ref[...] = both_ref[first, :]
    out_c_ref[...] = both_ref[second, :]
    state, grad = whole_state(state_ref, 0), whole_state(state_ref, STATE)
    sx, sg = either(scaled, first), either(scaled, second)
    pick = (iota((HEADS, WIDE), 0) == iota((HEADS, WIDE), 1) >> 6).astype(F32)
    whole = jnp.sum(grad.astype(F32) * state.astype(F32), axis=0, keepdims=True) * either(wide, heads)
    whole = jnp.sum(pick * whole, axis=1, keepdims=True)
    from_state = matmul(either(maps, second), state)
    state_back = matmul(either(maps, first), grad)
    out_x_ref[...] = (either(wide, first) + either(wide, second) * state_back).astype(BF16)
    through_head = sum_heads(pick, sg.astype(F32) * from_state)
    through_tail = sum_heads(pick, sx.astype(F32) * state_back)
    one, two = iota((length, length), 0), iota((length, length), 1)
    out_d_ref[...] = (
        either(narrow, heads)
        + matmul(through_head, (one >= two).astype(F32), HIGHEST)
        + matmul(through_tail, (one < two).astype(F32), HIGHEST)
        + whole
    )


def struct(shape, dtype):
    return jax.ShapeDtypeStruct(shape, dtype)


def call(kernel, out, operands, name, specs=None, scratch=(), flops=0, moved=0, limit=24):
    return pl.pallas_call(
        kernel,
        out_shape=out,
        in_specs=specs or [VMEM] * len(operands),
        out_specs=jax.tree.map(lambda _: VMEM, out),
        scratch_shapes=list(scratch),
        cost_estimate=pl.CostEstimate(flops=flops, bytes_accessed=moved, transcendentals=0),
        compiler_params=pltpu.CompilerParams(vmem_limit_bytes=limit * 2**20),
        name=name,
    )(*operands)


def local(inputs, log_decay, b_proj, c_proj, grad_out, w_bc):
    length = inputs.shape[0]
    width = w_bc.shape[2]
    block = [
        pltpu.with_memory_space_constraint(part, pltpu.HBM)
        for part in (log_decay, inputs, grad_out, b_proj, c_proj)
    ]
    held = [pltpu.VMEM(part.shape, part.dtype) for part in block]
    near = call(
        states_kernel,
        struct((LO, NEAR, LANES), BF16),
        block,
        "states",
        specs=[HBM] * 5,
        scratch=held + [pltpu.SemaphoreType.DMA((5,))],
        flops=4 * length * N * WIDE,
        moved=2**20,
    )
    near = lax.all_to_all(near, "lo", 0, 0, axis_index_groups=[NEAR_ORDER])
    inside = (
        struct((2 * length + HEADS, WIDE), F32),
        struct((2 * length + HEADS, N), F32),
        struct((2 * length, WIDE), BF16),
        struct((2 * length, N), BF16),
    )
    scratch = held + [pltpu.SemaphoreType.DMA((5,))]
    far, *before = call(
        segment_kernel,
        (struct((HI, FAR, LANES), BF16),) + inside,
        [near] + block,
        "segment",
        specs=[VMEM] + [HBM] * 5,
        scratch=scratch,
        moved=2**19,
    )
    far = lax.all_to_all(far, "hi", 0, 0, axis_index_groups=[FAR_ORDER])
    states, *after = call(
        entering_kernel,
        (struct((LO, 2 * STATE, LANES), BF16),) + inside,
        [far, near] + block,
        "entering",
        specs=[VMEM] * 2 + [HBM] * 5,
        scratch=scratch,
        moved=2**19,
    )
    states = lax.all_to_all(states, "lo", 0, 0, axis_index_groups=[BACK_ORDER])
    both, keep, send = call(
        tokens_kernel,
        (
            struct((2 * length, N), BF16),
            struct((length // 2, width), BF16),
            struct((length // 2, width), BF16),
        ),
        (states, before[1], before[2], after[1], after[2], w_bc.reshape(2 * N, width)),
        "tokens",
        flops=2**29,
        moved=4 * 2**20,
    )
    grad_inputs, grad_decay, grad_b, grad_c = call(
        carried_kernel,
        (
            struct((length, WIDE), BF16),
            struct((HEADS, length), F32),
            struct((length, N), BF16),
            struct((length, N), BF16),
        ),
        (states, both, *before, *after),
        "carried",
        flops=2**28,
        moved=2 * 2**20,
    )
    other = lax.ppermute(send, "core", [(0, 1), (1, 0)])
    rest = (grad_inputs, grad_decay, grad_b, grad_c)
    other, (grad_inputs, grad_decay, grad_b, grad_c) = lax.optimization_barrier((other, rest))
    pair = (keep.astype(F32) + other.astype(F32)).astype(BF16)
    blocks = pair.reshape(4, length // 8, width)
    blocks = lax.all_to_all(blocks, "x", 0, 0, axis_index_groups=[X_ORDER])
    grad_tokens = jnp.sum(blocks.astype(F32), axis=0).astype(BF16)
    return grad_inputs, grad_decay, grad_b, grad_c, grad_tokens


def solution(mesh):
    fine = Mesh(mesh.devices.reshape(HI, LO, 4, 2), ("hi", "lo", "x", "core"))
    ctx, head = ("hi", "lo"), ("x", "core")
    return jax.shard_map(
        local,
        mesh=fine,
        in_specs=(P(ctx, head), P(head, ctx), P(ctx, head), P(ctx, head), P(ctx, head), P(None, head, None)),
        out_specs=(P(ctx, head), P(head, ctx), P(ctx, head), P(ctx, head), P(ctx + head, None)),
        check_vma=False,
    )
```

```python
import functools

import jax
import jax.numpy as jnp
from jax import lax
from jax.experimental import pallas as pl
from jax.experimental.pallas import tpu as pltpu
from jax.sharding import Mesh, PartitionSpec as P

F32 = jnp.float32
BF16 = jnp.bfloat16
P_SIZE = 64
N = 128
HEADS = 8
WIDE = HEADS * P_SIZE
LO = 8
HI = 8
LANES = 128
ROWS = N // LO
HIGHEST = lax.Precision.HIGHEST
GROUPS = WIDE // LANES
STATE = GROUPS * ROWS
NEAR = 2 * STATE + 8
FAR = STATE + 8
EARLY = 3
NEAR_ORDER = [7, 6, 5, 4, 3, 2, 1, 0]
FAR_ORDER = [4, 5, 6, 7, 0, 1, 2, 3]
BACK_ORDER = [6, 7, 0, 1, 2, 3, 4, 5]
X_ORDER = [2, 3, 0, 1]
NEAR_ORDER_OF = [NEAR_ORDER.index(k) for k in range(LO)]
VMEM = pl.BlockSpec(memory_space=pltpu.VMEM)
HBM = pl.BlockSpec(memory_space=pltpu.HBM)


def iota(shape, axis):
    return lax.broadcasted_iota(jnp.int32, shape, axis)


def matmul(a, b, precision=None):
    return lax.dot_general(
        a, b, (((1,), (0,)), ((), ())), precision=precision, preferred_element_type=F32
    )


def matmul_nt(a, b, precision=None):
    return lax.dot_general(
        a, b, (((1,), (1,)), ((), ())), precision=precision, preferred_element_type=F32
    )


def matmul_tn(a, b):
    return lax.dot_general(a, b, (((0,), (0,)), ((), ())), preferred_element_type=F32)


def three_parts(values):
    first = values.astype(BF16).astype(F32)
    rest = values - first
    second = rest.astype(BF16).astype(F32)
    return jnp.concatenate([first, second, rest - second], axis=0).astype(BF16)


def cumulative(rate):
    length = rate.shape[1]
    upper = (iota((length, length), 0) <= iota((length, length), 1)).astype(BF16)
    rows = matmul(three_parts(rate), upper)
    rows = rows[0:HEADS] + rows[HEADS : 2 * HEADS] + rows[2 * HEADS : 3 * HEADS]
    return rows, three_parts(rows)


def widen(parts):
    part, column = iota((3 * HEADS, WIDE + LANES), 0), iota((3 * HEADS, WIDE + LANES), 1)
    of_head = jnp.logical_and((part & 7) == (column >> 6), column < WIDE)
    pick = jnp.logical_or(of_head, column - WIDE == part)
    return matmul_tn(parts, pick.astype(BF16))


def split_three(row):
    lane = iota(row.shape, 1)
    first = row.astype(BF16).astype(F32)
    rest = row - first
    second = rest.astype(BF16).astype(F32)
    third = rest - second
    parts = jnp.where(lane < HEADS, first, jnp.where(lane < 2 * HEADS, second, third))
    return jnp.where(lane < 3 * HEADS, parts, 0.0).astype(BF16)


def join_three(rows):
    lane, column = iota((LANES, WIDE), 0), iota((LANES, WIDE), 1)
    pick = jnp.logical_and((lane & 7) == (column >> 6), lane < 3 * HEADS)
    return matmul(rows, pick.astype(BF16))


def start_copies(sources, targets, sems):
    copies = [
        pltpu.make_async_copy(source, target, sems.at[k])
        for k, (source, target) in enumerate(zip(sources, targets))
    ]
    for copy in copies:
        copy.start()
    return copies


def states_kernel(rate_in, x_in, g_in, b_in, c_in, out_ref, rate_ref, x_ref, g_ref, b_ref, c_ref, sems):
    copies = start_copies(
        (rate_in, x_in, g_in, b_in, c_in), (rate_ref, x_ref, g_ref, b_ref, c_ref), sems
    )
    copies[0].wait()
    _, parts = cumulative(rate_ref[...])
    wide = widen(parts)
    length = wide.shape[0]
    last = wide[length - 1 : length, 0:WIDE]
    total = wide[length - 1 : length, WIDE : WIDE + LANES].astype(BF16)
    total = jnp.broadcast_to(total, (NEAR - 2 * STATE, LANES))
    wide = wide[:, 0:WIDE]
    tail = jnp.exp(last - wide)
    head = jnp.exp(wide)
    for copy in copies[1:]:
        copy.wait()
    scaled_inputs = (x_ref[...].astype(F32) * tail).astype(BF16)
    scaled_grads = (g_ref[...].astype(F32) * head).astype(BF16)
    state = matmul_tn(b_ref[...], scaled_inputs).astype(BF16)
    grad = matmul_tn(c_ref[...], scaled_grads).astype(BF16)
    for place, block in enumerate(NEAR_ORDER):
        rows = slice(block * ROWS, (block + 1) * ROWS)
        for k in range(GROUPS):
            at = slice(k * LANES, (k + 1) * LANES)
            out_ref[place, k * ROWS : (k + 1) * ROWS, :] = state[rows, at]
            out_ref[place, STATE + k * ROWS : STATE + (k + 1) * ROWS, :] = grad[rows, at]
        out_ref[place, 2 * STATE : NEAR, :] = total


def totals_of(ref, row):
    rows = [ref[k, row : ref.shape[1], :].astype(F32)[0:1] for k in range(ref.shape[0])]
    rows = jnp.concatenate(rows, axis=0)
    return rows, join_three(rows.astype(BF16))


def chunk_decays(wide):
    decay = jnp.exp(wide)
    return [
        jnp.concatenate(
            [
                jnp.broadcast_to(decay[k : k + 1, j * LANES : (j + 1) * LANES], (ROWS, LANES))
                for j in range(GROUPS)
            ],
            axis=0,
        )
        for k in range(decay.shape[0])
    ]


def block_body(
    rate_in,
    x_in,
    g_in,
    b_in,
    c_in,
    w_in,
    wide_ref,
    narrow_ref,
    scaled_ref,
    maps_ref,
    w_ref,
    rate_ref,
    x_ref,
    g_ref,
    b_ref,
    c_ref,
    sems,
):
    copies = start_copies(
        (rate_in, x_in, g_in, b_in, c_in), (rate_ref, x_ref, g_ref, b_ref, c_ref), sems
    )
    fetch = pltpu.make_async_copy(w_in, w_ref, sems.at[len(copies)])
    fetch.start()
    for copy in copies:
        copy.wait()
    rows, parts = cumulative(rate_ref[...])
    columns = jnp.transpose(rows)
    length = columns.shape[0]
    wide = widen(parts)[:, 0:WIDE]
    last = wide[length - 1 : length]
    tail = jnp.exp(last - wide)
    wide_ref[length : 2 * length, :] = tail
    wide_ref[2 * length : 2 * length + 8, :] = jnp.broadcast_to(jnp.exp(last), (8, WIDE))
    scaled_ref[0:length, :] = (x_ref[...].astype(F32) * tail).astype(BF16)
    scaled_ref[length : 2 * length, :] = (g_ref[...].astype(F32) * jnp.exp(wide)).astype(BF16)
    b, c = b_ref[...], c_ref[...]
    maps_ref[0:length, :] = b
    maps_ref[length : 2 * length, :] = c
    scores = matmul_nt(b, c)
    source, target = iota((length, length), 0), iota((length, length), 1)
    lower = source <= target
    before = source < target
    after = (source >= target).astype(BF16)
    lane = iota((length, LANES), 1)
    grad_scores = jnp.zeros((length, length), F32)
    decay_rows = []
    for pair in range(HEADS // 2):
        at = slice(pair * LANES, (pair + 1) * LANES)
        x_pair, g_pair = x_ref[:, at], g_ref[:, at]
        weights, masked = [], []
        for side in range(2):
            head = 2 * pair + side
            mine = (lane < P_SIZE) if side == 0 else (lane >= P_SIZE)
            x_mine = jnp.where(mine, x_pair, jnp.zeros_like(x_pair))
            g_mine = jnp.where(mine, g_pair, jnp.zeros_like(g_pair))
            gap = rows[head : head + 1, :] - columns[:, head : head + 1]
            decay = jnp.where(lower, jnp.exp(jnp.where(lower, gap, 0.0)), 0.0)
            grad_weights = matmul_nt(x_mine, g_pair)
            weight = scores * decay
            grad_scores = grad_scores + grad_weights * decay
            product = (grad_weights * weight).astype(BF16)
            through = matmul(product, after)
            decay_rows.append(jnp.sum(jnp.where(before, through, 0.0), axis=0, keepdims=True))
            weights.append(weight.astype(BF16))
            masked.append(g_mine)
        wide_ref[0:length, at] = matmul(jnp.concatenate(weights, axis=1), jnp.concatenate(masked, axis=0))
    narrow_ref[2 * length : 2 * length + HEADS, :] = jnp.concatenate(decay_rows, axis=0)
    narrow_ref[0:length, :] = matmul(grad_scores.astype(BF16), c)
    narrow_ref[length : 2 * length, :] = matmul(jnp.transpose(grad_scores).astype(BF16), b)
    fetch.wait()


def segment_kernel(in_ref, rate_in, x_in, g_in, b_in, c_in, w_in, out_ref, *rest):
    me = lax.axis_index("hi")
    rows, wide = totals_of(in_ref, 2 * STATE)
    decay = chunk_decays(wide)
    state = jnp.zeros((STATE, LANES), F32)
    grad = jnp.zeros((STATE, LANES), F32)
    for k in NEAR_ORDER_OF:
        state = decay[k] * state + in_ref[k, 0:STATE, :].astype(F32)
    for j in reversed(NEAR_ORDER_OF):
        grad = decay[j] * grad + in_ref[j, STATE : 2 * STATE, :].astype(F32)
    lane, other = iota((LANES, LANES), 0), iota((LANES, LANES), 1)
    fold = jnp.logical_and((lane & 7) == (other & 7), lane < 3 * HEADS).astype(BF16)
    total = jnp.sum(matmul(rows.astype(BF16), fold), axis=0, keepdims=True)
    total = jnp.broadcast_to(split_three(total), (FAR - STATE, LANES))
    state = state.astype(BF16)
    grad = grad.astype(BF16)
    for k, segment in enumerate(FAR_ORDER):
        out_ref[k, 0:STATE, :] = jnp.where(segment > me, state, grad)
        out_ref[k, STATE:FAR, :] = total

    @pl.when(me < EARLY)
    def _():
        block_body(rate_in, x_in, g_in, b_in, c_in, w_in, *rest)


def entering_kernel(far_ref, near_ref, rate_in, x_in, g_in, b_in, c_in, w_in, out_ref, *rest):
    me = lax.axis_index("hi")
    far = chunk_decays(totals_of(far_ref, STATE)[1])
    near = chunk_decays(totals_of(near_ref, 2 * STATE)[1])
    state = jnp.zeros((STATE, LANES), F32)
    grad = jnp.zeros((STATE, LANES), F32)
    for k in range(HI):
        at = FAR_ORDER.index(k)
        new = far[at] * state + far_ref[at, 0:STATE, :].astype(F32)
        state = jnp.where(k < me, new, state)
        j = HI - 1 - k
        at = FAR_ORDER.index(j)
        new = far[at] * grad + far_ref[at, 0:STATE, :].astype(F32)
        grad = jnp.where(j > me, new, grad)
    for k in range(LO):
        at = NEAR_ORDER.index(k)
        out_ref[BACK_ORDER.index(k), 0:STATE, :] = state.astype(BF16)
        state = near[at] * state + near_ref[at, 0:STATE, :].astype(F32)
        k = LO - 1 - k
        j = NEAR_ORDER.index(k)
        out_ref[BACK_ORDER.index(k), STATE : 2 * STATE, :] = grad.astype(BF16)
        grad = near[j] * grad + near_ref[j, STATE : 2 * STATE, :].astype(F32)

    @pl.when(me >= EARLY)
    def _():
        block_body(rate_in, x_in, g_in, b_in, c_in, w_in, *rest)


def whole_state(ref, row):
    parts = []
    for k in range(GROUPS):
        at = slice(row + k * ROWS, row + (k + 1) * ROWS)
        chunks = [ref[BACK_ORDER.index(block), at, :] for block in range(LO)]
        parts.append(jnp.concatenate(chunks, axis=0))
    return jnp.concatenate(parts, axis=1)


def either(pair, at):
    return jnp.where(lax.axis_index("hi") < EARLY, pair[0][at, :], pair[1][at, :])


def tokens_kernel(
    state_ref, narrow_a, scaled_a, w_a, narrow_b, scaled_b, w_b, both_ref, keep_ref, send_ref
):
    narrow, scaled = (narrow_a, narrow_b), (scaled_a, scaled_b)
    length = scaled_a.shape[0] // 2
    first, second = slice(0, length), slice(length, 2 * length)
    grad_c = matmul_nt(either(scaled, second), whole_state(state_ref, 0))
    grad_b = matmul_nt(either(scaled, first), whole_state(state_ref, STATE))
    grad_c = (grad_c + either(narrow, second)).astype(BF16)
    grad_b = (grad_b + either(narrow, first)).astype(BF16)
    both_ref[first, :] = grad_b
    both_ref[second, :] = grad_c
    both = jnp.concatenate([grad_b, grad_c], axis=1)
    rows = length // 8
    even = jnp.concatenate([both[2 * k * rows : (2 * k + 1) * rows] for k in X_ORDER], axis=0)
    odd = jnp.concatenate([both[(2 * k + 1) * rows : (2 * k + 2) * rows] for k in X_ORDER], axis=0)
    here = lax.axis_index("core") == 0
    keep = jnp.where(here, even, odd)
    send = jnp.where(here, odd, even)
    both = jnp.concatenate([keep, send], axis=0)
    half = length // 2
    step = 512

    def times(w_ref):
        for k in range(w_ref.shape[1] // step):
            at = slice(k * step, (k + 1) * step)
            part = matmul(both, w_ref[:, at]).astype(BF16)
            keep_ref[:, at] = part[:half]
            send_ref[:, at] = part[half:]

    early = lax.axis_index("hi") < EARLY
    pl.when(early)(lambda: times(w_a))
    pl.when(jnp.logical_not(early))(lambda: times(w_b))


def sum_heads(pick, values):
    pick = pick.astype(BF16)
    high = values.astype(BF16)
    low = (values - high.astype(F32)).astype(BF16)
    return matmul_nt(pick, high) + matmul_nt(pick, low)


def carried_kernel(
    state_ref,
    both_ref,
    wide_a,
    narrow_a,
    scaled_a,
    maps_a,
    wide_b,
    narrow_b,
    scaled_b,
    maps_b,
    out_x_ref,
    out_d_ref,
    out_b_ref,
    out_c_ref,
):
    wide, narrow = (wide_a, wide_b), (narrow_a, narrow_b)
    scaled, maps = (scaled_a, scaled_b), (maps_a, maps_b)
    length = out_b_ref.shape[0]
    first, second = slice(0, length), slice(length, 2 * length)
    heads = slice(2 * length, 2 * length + HEADS)
    out_b_ref[...] = both_ref[first, :]
    out_c_ref[...] = both_ref[second, :]
    state, grad = whole_state(state_ref, 0), whole_state(state_ref, STATE)
    sx, sg = either(scaled, first), either(scaled, second)
    pick = (iota((HEADS, WIDE), 0) == iota((HEADS, WIDE), 1) >> 6).astype(F32)
    whole = jnp.sum(grad.astype(F32) * state.astype(F32), axis=0, keepdims=True) * either(wide, heads)
    whole = jnp.sum(pick * whole, axis=1, keepdims=True)
    from_state = matmul(either(maps, second), state)
    state_back = matmul(either(maps, first), grad)
    out_x_ref[...] = (either(wide, first) + either(wide, second) * state_back).astype(BF16)
    through_head = sum_heads(pick, sg.astype(F32) * from_state)
    through_tail = sum_heads(pick, sx.astype(F32) * state_back)
    one, two = iota((length, length), 0), iota((length, length), 1)
    out_d_ref[...] = (
        either(narrow, heads)
        + matmul(through_head, (one >= two).astype(F32), HIGHEST)
        + matmul(through_tail, (one < two).astype(F32), HIGHEST)
        + whole
    )


def struct(shape, dtype):
    return jax.ShapeDtypeStruct(shape, dtype)


def call(kernel, out, operands, name, specs=None, scratch=(), flops=0, moved=0, limit=24):
    return pl.pallas_call(
        kernel,
        out_shape=out,
        in_specs=specs or [VMEM] * len(operands),
        out_specs=jax.tree.map(lambda _: VMEM, out),
        scratch_shapes=list(scratch),
        cost_estimate=pl.CostEstimate(flops=flops, bytes_accessed=moved, transcendentals=0),
        compiler_params=pltpu.CompilerParams(vmem_limit_bytes=limit * 2**20),
        name=name,
    )(*operands)


def local(inputs, log_decay, b_proj, c_proj, grad_out, w_bc):
    length = inputs.shape[0]
    width = w_bc.shape[2]
    block = [
        pltpu.with_memory_space_constraint(part, pltpu.HBM)
        for part in (log_decay, inputs, grad_out, b_proj, c_proj)
    ]
    held = [pltpu.VMEM(part.shape, part.dtype) for part in block]
    near = call(
        states_kernel,
        struct((LO, NEAR, LANES), BF16),
        block,
        "states",
        specs=[HBM] * 5,
        scratch=held + [pltpu.SemaphoreType.DMA((5,))],
        flops=4 * length * N * WIDE,
        moved=2**20,
    )
    near = lax.all_to_all(near, "lo", 0, 0, axis_index_groups=[NEAR_ORDER])
    inside = (
        struct((2 * length + HEADS, WIDE), F32),
        struct((2 * length + HEADS, N), F32),
        struct((2 * length, WIDE), BF16),
        struct((2 * length, N), BF16),
        struct((2 * N, width), BF16),
    )
    scratch = held + [pltpu.SemaphoreType.DMA((6,))]
    block.append(pltpu.with_memory_space_constraint(w_bc.reshape(2 * N, width), pltpu.HBM))
    far, *before = call(
        segment_kernel,
        (struct((HI, FAR, LANES), BF16),) + inside,
        [near] + block,
        "segment",
        specs=[VMEM] + [HBM] * 6,
        scratch=scratch,
        moved=2**19,
    )
    far = lax.all_to_all(far, "hi", 0, 0, axis_index_groups=[FAR_ORDER])
    states, *after = call(
        entering_kernel,
        (struct((LO, 2 * STATE, LANES), BF16),) + inside,
        [far, near] + block,
        "entering",
        specs=[VMEM] * 2 + [HBM] * 6,
        scratch=scratch,
        moved=2**19,
    )
    states = lax.all_to_all(states, "lo", 0, 0, axis_index_groups=[BACK_ORDER])
    both, keep, send = call(
        tokens_kernel,
        (
            struct((2 * length, N), BF16),
            struct((length // 2, width), BF16),
            struct((length // 2, width), BF16),
        ),
        (states, before[1], before[2], before[4], after[1], after[2], after[4]),
        "tokens",
        flops=2**29,
        moved=4 * 2**20,
    )
    grad_inputs, grad_decay, grad_b, grad_c = call(
        carried_kernel,
        (
            struct((length, WIDE), BF16),
            struct((HEADS, length), F32),
            struct((length, N), BF16),
            struct((length, N), BF16),
        ),
        (states, both, *before[:4], *after[:4]),
        "carried",
        flops=2**28,
        moved=2 * 2**20,
    )
    other = lax.ppermute(send, "core", [(0, 1), (1, 0)])
    rest = (grad_inputs, grad_decay, grad_b, grad_c)
    other, (grad_inputs, grad_decay, grad_b, grad_c) = lax.optimization_barrier((other, rest))
    pair = (keep.astype(F32) + other.astype(F32)).astype(BF16)
    blocks = pair.reshape(4, length // 8, width)
    blocks = lax.all_to_all(blocks, "x", 0, 0, axis_index_groups=[X_ORDER])
    grad_tokens = jnp.sum(blocks.astype(F32), axis=0).astype(BF16)
    return grad_inputs, grad_decay, grad_b, grad_c, grad_tokens


def solution(mesh):
    fine = Mesh(mesh.devices.reshape(HI, LO, 4, 2), ("hi", "lo", "x", "core"))
    ctx, head = ("hi", "lo"), ("x", "core")
    return jax.shard_map(
        local,
        mesh=fine,
        in_specs=(P(ctx, head), P(head, ctx), P(ctx, head), P(ctx, head), P(ctx, head), P(None, head, None)),
        out_specs=(P(ctx, head), P(head, ctx), P(ctx, head), P(ctx, head), P(ctx + head, None)),
        check_vma=False,
    )
```

```python
import functools

import jax
import jax.numpy as jnp
from jax import lax
from jax.experimental import pallas as pl
from jax.experimental.pallas import tpu as pltpu
from jax.sharding import Mesh, PartitionSpec as P

F32 = jnp.float32
BF16 = jnp.bfloat16
P_SIZE = 64
N = 128
HEADS = 8
WIDE = HEADS * P_SIZE
LO = 8
HI = 8
LANES = 128
ROWS = N // LO
HIGHEST = lax.Precision.HIGHEST
GROUPS = WIDE // LANES
STATE = GROUPS * ROWS
NEAR = 2 * STATE + 8
FAR = STATE + 8
EARLY = 3
NEAR_ORDER = [7, 6, 5, 4, 3, 2, 1, 0]
FAR_ORDER = [4, 5, 6, 7, 0, 1, 2, 3]
BACK_ORDER = [6, 7, 0, 1, 2, 3, 4, 5]
X_ORDER = [2, 3, 0, 1]
NEAR_ORDER_OF = [NEAR_ORDER.index(k) for k in range(LO)]
VMEM = pl.BlockSpec(memory_space=pltpu.VMEM)
HBM = pl.BlockSpec(memory_space=pltpu.HBM)


def iota(shape, axis):
    return lax.broadcasted_iota(jnp.int32, shape, axis)


def matmul(a, b, precision=None):
    return lax.dot_general(
        a, b, (((1,), (0,)), ((), ())), precision=precision, preferred_element_type=F32
    )


def matmul_nt(a, b, precision=None):
    return lax.dot_general(
        a, b, (((1,), (1,)), ((), ())), precision=precision, preferred_element_type=F32
    )


def matmul_tn(a, b):
    return lax.dot_general(a, b, (((0,), (0,)), ((), ())), preferred_element_type=F32)


def three_parts(values):
    first = values.astype(BF16).astype(F32)
    rest = values - first
    second = rest.astype(BF16).astype(F32)
    return jnp.concatenate([first, second, rest - second], axis=0).astype(BF16)


def cumulative(rate):
    length = rate.shape[1]
    upper = (iota((length, length), 0) <= iota((length, length), 1)).astype(BF16)
    rows = matmul(three_parts(rate), upper)
    rows = rows[0:HEADS] + rows[HEADS : 2 * HEADS] + rows[2 * HEADS : 3 * HEADS]
    return rows, three_parts(rows)


def widen(parts):
    part, column = iota((3 * HEADS, WIDE + LANES), 0), iota((3 * HEADS, WIDE + LANES), 1)
    of_head = jnp.logical_and((part & 7) == (column >> 6), column < WIDE)
    pick = jnp.logical_or(of_head, column - WIDE == part)
    return matmul_tn(parts, pick.astype(BF16))


def split_three(row):
    lane = iota(row.shape, 1)
    first = row.astype(BF16).astype(F32)
    rest = row - first
    second = rest.astype(BF16).astype(F32)
    third = rest - second
    parts = jnp.where(lane < HEADS, first, jnp.where(lane < 2 * HEADS, second, third))
    return jnp.where(lane < 3 * HEADS, parts, 0.0).astype(BF16)


def join_three(rows):
    lane, column = iota((LANES, WIDE), 0), iota((LANES, WIDE), 1)
    pick = jnp.logical_and((lane & 7) == (column >> 6), lane < 3 * HEADS)
    return matmul(rows, pick.astype(BF16))


def start_copies(sources, targets, sems):
    copies = [
        pltpu.make_async_copy(source, target, sems.at[k])
        for k, (source, target) in enumerate(zip(sources, targets))
    ]
    for copy in copies:
        copy.start()
    return copies


def states_kernel(rate_in, x_in, g_in, b_in, c_in, out_ref, rate_ref, x_ref, g_ref, b_ref, c_ref, sems):
    copies = start_copies(
        (rate_in, x_in, g_in, b_in, c_in), (rate_ref, x_ref, g_ref, b_ref, c_ref), sems
    )
    copies[0].wait()
    _, parts = cumulative(rate_ref[...])
    wide = widen(parts)
    length = wide.shape[0]
    last = wide[length - 1 : length, 0:WIDE]
    total = wide[length - 1 : length, WIDE : WIDE + LANES].astype(BF16)
    total = jnp.broadcast_to(total, (NEAR - 2 * STATE, LANES))
    wide = wide[:, 0:WIDE]
    tail = jnp.exp(last - wide)
    head = jnp.exp(wide)
    for copy in copies[1:]:
        copy.wait()
    scaled_inputs = (x_ref[...].astype(F32) * tail).astype(BF16)
    scaled_grads = (g_ref[...].astype(F32) * head).astype(BF16)
    state = matmul_tn(b_ref[...], scaled_inputs).astype(BF16)
    grad = matmul_tn(c_ref[...], scaled_grads).astype(BF16)
    for place, block in enumerate(NEAR_ORDER):
        rows = slice(block * ROWS, (block + 1) * ROWS)
        for k in range(GROUPS):
            at = slice(k * LANES, (k + 1) * LANES)
            out_ref[place, k * ROWS : (k + 1) * ROWS, :] = state[rows, at]
            out_ref[place, STATE + k * ROWS : STATE + (k + 1) * ROWS, :] = grad[rows, at]
        out_ref[place, 2 * STATE : NEAR, :] = total


def totals_of(ref, row):
    rows = [ref[k, row : ref.shape[1], :].astype(F32)[0:1] for k in range(ref.shape[0])]
    rows = jnp.concatenate(rows, axis=0)
    return rows, join_three(rows.astype(BF16))


def chunk_decays(wide):
    decay = jnp.exp(wide)
    return [
        jnp.concatenate(
            [
                jnp.broadcast_to(decay[k : k + 1, j * LANES : (j + 1) * LANES], (ROWS, LANES))
                for j in range(GROUPS)
            ],
            axis=0,
        )
        for k in range(decay.shape[0])
    ]


def block_body(
    rate_in,
    x_in,
    g_in,
    b_in,
    c_in,
    w_in,
    wide_ref,
    narrow_ref,
    scaled_ref,
    maps_ref,
    w_ref,
    rate_ref,
    x_ref,
    g_ref,
    b_ref,
    c_ref,
    sems,
):
    copies = start_copies(
        (rate_in, x_in, g_in, b_in, c_in), (rate_ref, x_ref, g_ref, b_ref, c_ref), sems
    )
    fetch = pltpu.make_async_copy(w_in, w_ref, sems.at[len(copies)])
    fetch.start()
    for copy in copies:
        copy.wait()
    rows, parts = cumulative(rate_ref[...])
    columns = jnp.transpose(rows)
    length = columns.shape[0]
    wide = widen(parts)[:, 0:WIDE]
    last = wide[length - 1 : length]
    tail = jnp.exp(last - wide)
    wide_ref[length : 2 * length, :] = tail
    wide_ref[2 * length : 2 * length + 8, :] = jnp.broadcast_to(jnp.exp(last), (8, WIDE))
    scaled_ref[0:length, :] = (x_ref[...].astype(F32) * tail).astype(BF16)
    scaled_ref[length : 2 * length, :] = (g_ref[...].astype(F32) * jnp.exp(wide)).astype(BF16)
    b, c = b_ref[...], c_ref[...]
    maps_ref[0:length, :] = b
    maps_ref[length : 2 * length, :] = c
    scores = matmul_nt(b, c)
    source, target = iota((length, length), 0), iota((length, length), 1)
    lower = source <= target
    before = source < target
    after = (source >= target).astype(BF16)
    lane = iota((length, LANES), 1)
    grad_scores = jnp.zeros((length, length), F32)
    decay_rows = []
    for pair in range(HEADS // 2):
        at = slice(pair * LANES, (pair + 1) * LANES)
        x_pair, g_pair = x_ref[:, at], g_ref[:, at]
        weights, masked = [], []
        for side in range(2):
            head = 2 * pair + side
            mine = (lane < P_SIZE) if side == 0 else (lane >= P_SIZE)
            x_mine = jnp.where(mine, x_pair, jnp.zeros_like(x_pair))
            g_mine = jnp.where(mine, g_pair, jnp.zeros_like(g_pair))
            gap = rows[head : head + 1, :] - columns[:, head : head + 1]
            decay = jnp.where(lower, jnp.exp(jnp.where(lower, gap, 0.0)), 0.0)
            grad_weights = matmul_nt(x_mine, g_pair)
            weight = scores * decay
            grad_scores = grad_scores + grad_weights * decay
            product = (grad_weights * weight).astype(BF16)
            through = matmul(product, after)
            decay_rows.append(jnp.sum(jnp.where(before, through, 0.0), axis=0, keepdims=True))
            weights.append(weight.astype(BF16))
            masked.append(g_mine)
        wide_ref[0:length, at] = matmul(jnp.concatenate(weights, axis=1), jnp.concatenate(masked, axis=0))
    narrow_ref[2 * length : 2 * length + HEADS, :] = jnp.concatenate(decay_rows, axis=0)
    narrow_ref[0:length, :] = matmul(grad_scores.astype(BF16), c)
    narrow_ref[length : 2 * length, :] = matmul(jnp.transpose(grad_scores).astype(BF16), b)
    fetch.wait()


def segment_kernel(in_ref, rate_in, x_in, g_in, b_in, c_in, w_in, out_ref, *rest):
    me = lax.axis_index("hi")
    rows, wide = totals_of(in_ref, 2 * STATE)
    decay = chunk_decays(wide)
    state = jnp.zeros((STATE, LANES), F32)
    grad = jnp.zeros((STATE, LANES), F32)
    for k in NEAR_ORDER_OF:
        state = decay[k] * state + in_ref[k, 0:STATE, :].astype(F32)
    for j in reversed(NEAR_ORDER_OF):
        grad = decay[j] * grad + in_ref[j, STATE : 2 * STATE, :].astype(F32)
    lane, other = iota((LANES, LANES), 0), iota((LANES, LANES), 1)
    fold = jnp.logical_and((lane & 7) == (other & 7), lane < 3 * HEADS).astype(BF16)
    total = jnp.sum(matmul(rows.astype(BF16), fold), axis=0, keepdims=True)
    total = jnp.broadcast_to(split_three(total), (FAR - STATE, LANES))
    state = state.astype(BF16)
    grad = grad.astype(BF16)
    for k, segment in enumerate(FAR_ORDER):
        out_ref[k, 0:STATE, :] = jnp.where(segment > me, state, grad)
        out_ref[k, STATE:FAR, :] = total

    @pl.when(me < EARLY)
    def _():
        block_body(rate_in, x_in, g_in, b_in, c_in, w_in, *rest)


def entering_kernel(far_ref, near_ref, rate_in, x_in, g_in, b_in, c_in, w_in, out_ref, *rest):
    me = lax.axis_index("hi")
    far = chunk_decays(totals_of(far_ref, STATE)[1])
    near = chunk_decays(totals_of(near_ref, 2 * STATE)[1])
    state = jnp.zeros((STATE, LANES), F32)
    grad = jnp.zeros((STATE, LANES), F32)
    for k in range(HI):
        at = FAR_ORDER.index(k)
        new = far[at] * state + far_ref[at, 0:STATE, :].astype(F32)
        state = jnp.where(k < me, new, state)
        j = HI - 1 - k
        at = FAR_ORDER.index(j)
        new = far[at] * grad + far_ref[at, 0:STATE, :].astype(F32)
        grad = jnp.where(j > me, new, grad)
    for k in range(LO):
        at = NEAR_ORDER.index(k)
        out_ref[BACK_ORDER.index(k), 0:STATE, :] = state.astype(BF16)
        state = near[at] * state + near_ref[at, 0:STATE, :].astype(F32)
        k = LO - 1 - k
        j = NEAR_ORDER.index(k)
        out_ref[BACK_ORDER.index(k), STATE : 2 * STATE, :] = grad.astype(BF16)
        grad = near[j] * grad + near_ref[j, STATE : 2 * STATE, :].astype(F32)

    @pl.when(me >= EARLY)
    def _():
        block_body(rate_in, x_in, g_in, b_in, c_in, w_in, *rest)


def whole_state(ref, row):
    parts = []
    for k in range(GROUPS):
        at = slice(row + k * ROWS, row + (k + 1) * ROWS)
        chunks = [ref[BACK_ORDER.index(block), at, :] for block in range(LO)]
        parts.append(jnp.concatenate(chunks, axis=0))
    return jnp.concatenate(parts, axis=1)


def either(pair, at):
    return jnp.where(lax.axis_index("hi") < EARLY, pair[0][at, :], pair[1][at, :])


def tokens_kernel(
    state_ref, narrow_a, scaled_a, w_a, narrow_b, scaled_b, w_b, both_ref, keep_ref, send_ref
):
    narrow, scaled = (narrow_a, narrow_b), (scaled_a, scaled_b)
    length = scaled_a.shape[0] // 2
    first, second = slice(0, length), slice(length, 2 * length)
    grad_c = matmul_nt(either(scaled, second), whole_state(state_ref, 0))
    grad_b = matmul_nt(either(scaled, first), whole_state(state_ref, STATE))
    grad_c = (grad_c + either(narrow, second)).astype(BF16)
    grad_b = (grad_b + either(narrow, first)).astype(BF16)
    both_ref[first, :] = grad_b
    both_ref[second, :] = grad_c
    both = jnp.concatenate([grad_b, grad_c], axis=1)
    rows = length // 8
    even = jnp.concatenate([both[2 * k * rows : (2 * k + 1) * rows] for k in X_ORDER], axis=0)
    odd = jnp.concatenate([both[(2 * k + 1) * rows : (2 * k + 2) * rows] for k in X_ORDER], axis=0)
    here = lax.axis_index("core") == 0
    keep = jnp.where(here, even, odd)
    send = jnp.where(here, odd, even)
    both = jnp.concatenate([keep, send], axis=0)
    half = length // 2
    step = 512

    def times(w_ref):
        for k in range(w_ref.shape[1] // step):
            at = slice(k * step, (k + 1) * step)
            part = matmul(both, w_ref[:, at]).astype(BF16)
            keep_ref[:, at] = part[:half]
            send_ref[:, at] = part[half:]

    early = lax.axis_index("hi") < EARLY
    pl.when(early)(lambda: times(w_a))
    pl.when(jnp.logical_not(early))(lambda: times(w_b))


def sum_heads(pick, values):
    pick = pick.astype(BF16)
    high = values.astype(BF16)
    low = (values - high.astype(F32)).astype(BF16)
    return matmul_nt(pick, high) + matmul_nt(pick, low)


def carried_kernel(
    state_ref,
    both_ref,
    wide_a,
    narrow_a,
    scaled_a,
    maps_a,
    wide_b,
    narrow_b,
    scaled_b,
    maps_b,
    out_x_ref,
    out_d_ref,
    out_b_ref,
    out_c_ref,
):
    wide, narrow = (wide_a, wide_b), (narrow_a, narrow_b)
    scaled, maps = (scaled_a, scaled_b), (maps_a, maps_b)
    length = out_b_ref.shape[0]
    first, second = slice(0, length), slice(length, 2 * length)
    heads = slice(2 * length, 2 * length + HEADS)
    out_b_ref[...] = both_ref[first, :]
    out_c_ref[...] = both_ref[second, :]
    state, grad = whole_state(state_ref, 0), whole_state(state_ref, STATE)
    sx, sg = either(scaled, first), either(scaled, second)
    pick = (iota((HEADS, WIDE), 0) == iota((HEADS, WIDE), 1) >> 6).astype(F32)
    whole = jnp.sum(grad.astype(F32) * state.astype(F32), axis=0, keepdims=True) * either(wide, heads)
    whole = jnp.sum(pick * whole, axis=1, keepdims=True)
    from_state = matmul(either(maps, second), state)
    state_back = matmul(either(maps, first), grad)
    out_x_ref[...] = (either(wide, first) + either(wide, second) * state_back).astype(BF16)
    through_head = sum_heads(pick, sg.astype(F32) * from_state)
    through_tail = sum_heads(pick, sx.astype(F32) * state_back)
    one, two = iota((length, length), 0), iota((length, length), 1)
    out_d_ref[...] = (
        either(narrow, heads)
        + matmul(through_head, (one >= two).astype(F32), HIGHEST)
        + matmul(through_tail, (one < two).astype(F32), HIGHEST)
        + whole
    )


def sum_kernel(in_ref, out_ref, sum_ref, sems):
    step = in_ref.shape[2] // 4
    copies = []
    for k in range(4):
        at = slice(k * step, (k + 1) * step)
        total = in_ref[0, :, at].astype(F32)
        for block in range(1, in_ref.shape[0]):
            total = total + in_ref[block, :, at].astype(F32)
        sum_ref[:, at] = total.astype(BF16)
        copy = pltpu.make_async_copy(sum_ref.at[:, at], out_ref.at[:, at], sems.at[k])
        copy.start()
        copies.append(copy)
    for copy in copies:
        copy.wait()


def struct(shape, dtype):
    return jax.ShapeDtypeStruct(shape, dtype)


def call(kernel, out, operands, name, specs=None, scratch=(), flops=0, moved=0, limit=24):
    return pl.pallas_call(
        kernel,
        out_shape=out,
        in_specs=specs or [VMEM] * len(operands),
        out_specs=jax.tree.map(lambda _: VMEM, out),
        scratch_shapes=list(scratch),
        cost_estimate=pl.CostEstimate(flops=flops, bytes_accessed=moved, transcendentals=0),
        compiler_params=pltpu.CompilerParams(vmem_limit_bytes=limit * 2**20),
        name=name,
    )(*operands)


def local(inputs, log_decay, b_proj, c_proj, grad_out, w_bc):
    length = inputs.shape[0]
    width = w_bc.shape[2]
    block = [
        pltpu.with_memory_space_constraint(part, pltpu.HBM)
        for part in (log_decay, inputs, grad_out, b_proj, c_proj)
    ]
    held = [pltpu.VMEM(part.shape, part.dtype) for part in block]
    near = call(
        states_kernel,
        struct((LO, NEAR, LANES), BF16),
        block,
        "states",
        specs=[HBM] * 5,
        scratch=held + [pltpu.SemaphoreType.DMA((5,))],
        flops=4 * length * N * WIDE,
        moved=2**20,
    )
    near = lax.all_to_all(near, "lo", 0, 0, axis_index_groups=[NEAR_ORDER])
    inside = (
        struct((2 * length + HEADS, WIDE), F32),
        struct((2 * length + HEADS, N), F32),
        struct((2 * length, WIDE), BF16),
        struct((2 * length, N), BF16),
        struct((2 * N, width), BF16),
    )
    scratch = held + [pltpu.SemaphoreType.DMA((6,))]
    block.append(pltpu.with_memory_space_constraint(w_bc.reshape(2 * N, width), pltpu.HBM))
    far, *before = call(
        segment_kernel,
        (struct((HI, FAR, LANES), BF16),) + inside,
        [near] + block,
        "segment",
        specs=[VMEM] + [HBM] * 6,
        scratch=scratch,
        moved=2**19,
    )
    far = lax.all_to_all(far, "hi", 0, 0, axis_index_groups=[FAR_ORDER])
    states, *after = call(
        entering_kernel,
        (struct((LO, 2 * STATE, LANES), BF16),) + inside,
        [far, near] + block,
        "entering",
        specs=[VMEM] * 2 + [HBM] * 6,
        scratch=scratch,
        moved=2**19,
    )
    states = lax.all_to_all(states, "lo", 0, 0, axis_index_groups=[BACK_ORDER])
    both, keep, send = call(
        tokens_kernel,
        (
            struct((2 * length, N), BF16),
            struct((length // 2, width), BF16),
            struct((length // 2, width), BF16),
        ),
        (states, before[1], before[2], before[4], after[1], after[2], after[4]),
        "tokens",
        flops=2**29,
        moved=4 * 2**20,
    )
    grad_inputs, grad_decay, grad_b, grad_c = call(
        carried_kernel,
        (
            struct((length, WIDE), BF16),
            struct((HEADS, length), F32),
            struct((length, N), BF16),
            struct((length, N), BF16),
        ),
        (states, both, *before[:4], *after[:4]),
        "carried",
        flops=2**28,
        moved=2 * 2**20,
    )
    other = lax.ppermute(send, "core", [(0, 1), (1, 0)])
    rest = (grad_inputs, grad_decay, grad_b, grad_c)
    other, (grad_inputs, grad_decay, grad_b, grad_c) = lax.optimization_barrier((other, rest))
    pair = (keep.astype(F32) + other.astype(F32)).astype(BF16)
    blocks = pair.reshape(4, length // 8, width)
    blocks = lax.all_to_all(blocks, "x", 0, 0, axis_index_groups=[X_ORDER])
    rows = length // 8
    grad_tokens = pl.pallas_call(
        sum_kernel,
        out_shape=pltpu.HBM((rows, width), BF16),
        in_specs=[VMEM],
        out_specs=HBM,
        scratch_shapes=[pltpu.VMEM((rows, width), BF16), pltpu.SemaphoreType.DMA((4,))],
        cost_estimate=pl.CostEstimate(flops=2**18, bytes_accessed=2**20, transcendentals=0),
        compiler_params=pltpu.CompilerParams(vmem_limit_bytes=8 * 2**20),
        name="sum",
    )(blocks)
    return grad_inputs, grad_decay, grad_b, grad_c, grad_tokens


def solution(mesh):
    fine = Mesh(mesh.devices.reshape(HI, LO, 4, 2), ("hi", "lo", "x", "core"))
    ctx, head = ("hi", "lo"), ("x", "core")
    return jax.shard_map(
        local,
        mesh=fine,
        in_specs=(P(ctx, head), P(head, ctx), P(ctx, head), P(ctx, head), P(ctx, head), P(None, head, None)),
        out_specs=(P(ctx, head), P(head, ctx), P(ctx, head), P(ctx, head), P(ctx + head, None)),
        check_vma=False,
    )
```
